1024 devices in a mesh: row: 32 (over z_lo, y, core), col: 32 (over x, z_hi).
Axes of the slice: x: 8, y: 8, z: 8 (z_hi: 4, z_lo: 2; z = z_hi * 2 + z_lo), core: 2. Of those that a mesh axis runs over, the one named last changes fastest.
Arguments:
- panel_blocks: float32 [256, 96, 128, 128], P('row', 'col'), may hold values from -1.5 to 1.5
- panel_cols: int32 [256, 96], replicated, may hold values from 0 to 7, as said below
- panel_count: int32 [256, 32], replicated, may hold values from 0 to 3
- product_cols: int32 [256, 96], replicated, may hold values from 0 to 7, as said below
- product_count: int32 [256, 32], replicated, may hold values from 0 to 3
Outputs:
- product: float32 [256, 96, 128, 128], P('row', 'col')
The draws below stay inside these ranges and needn't reach their ends.
Inputs may be any that keep to these rules, and one draw needn't show every extreme that they name: `panel_cols`: within one block row and one column group the 3 indices are distinct. `product_cols`: within one block row and one column group the 3 indices are distinct.
All inputs are finite; a program needn't handle non-finite values.
Results may differ from the reference program's by a relative error of at most 0.0003.
Values sent between devices are 32-bit elements; how exact they have to be, the bound alone decides.
A program may use at most 32 MiB of HBM per device.

```python
import jax
import jax.numpy as jnp
from jax import lax

BLOCK = 128
GROUP_ROWS = 8
SLOTS_A = 3
SLOTS_C = 3
STEPS = 2
GROUPS = 32
BLOCK_ROWS = 256


def distinct_columns(key, slots_each):
    scores = jax.random.randint(key, (BLOCK_ROWS, GROUPS, GROUP_ROWS), 0, 1 << 20) * GROUP_ROWS + jnp.arange(GROUP_ROWS, dtype=jnp.int32)
    ranking = jnp.argsort(scores, axis=-1)
    return ranking[:, :, :slots_each].reshape(BLOCK_ROWS, GROUPS * slots_each).astype(jnp.int32)


def live_counts(key, largest):
    entries = BLOCK_ROWS * GROUPS
    counts = jax.random.randint(key, (entries,), 0, largest + 1)
    positions = jax.random.randint(jax.random.fold_in(key, 5), (2,), 0, entries)
    partner_spot = (positions[0] + 1 + positions[1] % (entries - 1)) % entries
    counts = counts.at[positions[0]].set(largest).at[partner_spot].set(0)
    return counts.reshape(BLOCK_ROWS, GROUPS).astype(jnp.int32)


def draw_panel_cols(key, part):
    key = jax.random.fold_in(key, 11)
    return distinct_columns(key, SLOTS_A)


def draw_panel_count(key, part):
    key = jax.random.fold_in(key, 12)
    return live_counts(key, SLOTS_A)


def draw_product_cols(key, part):
    key = jax.random.fold_in(key, 13)
    return distinct_columns(key, SLOTS_C)


def draw_product_count(key, part):
    key = jax.random.fold_in(key, 14)
    return live_counts(key, SLOTS_C)


def block_levels(own_key, shape, shards, low, high):
    def one(axis_at, parts):
        draws = jax.random.uniform(jax.random.fold_in(jax.random.fold_in(own_key, 6), axis_at), (parts,), jnp.float32, low / len(shards), high / len(shards))
        return jnp.repeat(jnp.exp(draws), shape[axis_at] // parts).reshape((-1,) + (1,) * (len(shape) - axis_at - 1))

    level = one(*shards[0])
    for cut in shards[1:]:
        level = level * one(*cut)
    return level


def scatter_about(key, extent, spread, bound, pieces=(), kind=jnp.bfloat16):
    level = block_levels(key, extent, pieces, -0.22, 0.18) if pieces else 1.0
    values = jax.random.normal(key, extent, jnp.float32) * spread * level
    return jnp.minimum(jnp.maximum(values, -bound), bound).astype(kind)


def setup_inputs(seed: int = 0) -> dict:
    splits = jax.random.split(jax.random.key(seed), 6)
    panel_blocks = scatter_about(splits[0], (BLOCK_ROWS, GROUPS * SLOTS_A, BLOCK, BLOCK), 0.25, 1.5, ((0, 32), (1, 32)), jnp.float32)
    panel_cols = draw_panel_cols(jax.random.fold_in(splits[5], 71), 0)
    panel_count = draw_panel_count(jax.random.fold_in(splits[5], 71), 0)
    product_cols = draw_product_cols(jax.random.fold_in(splits[5], 71), 0)
    product_count = draw_product_count(jax.random.fold_in(splits[5], 71), 0)
    return dict(panel_blocks=panel_blocks, panel_cols=panel_cols, panel_count=panel_count, product_cols=product_cols, product_count=product_count)


FULL = lax.Precision.HIGHEST


def reference(panel_blocks, panel_cols, panel_count, product_cols, product_count):
    blocks = panel_blocks.reshape(BLOCK_ROWS, GROUPS, SLOTS_A, BLOCK, BLOCK)
    columns = panel_cols.reshape(BLOCK_ROWS, GROUPS, SLOTS_A)
    living = jnp.arange(SLOTS_A, dtype=jnp.int32)[None, None, :] < panel_count[:, :, None]
    wanted = product_cols.reshape(BLOCK_ROWS, GROUPS, SLOTS_C)
    kept_slots = jnp.arange(SLOTS_C, dtype=jnp.int32)[None, None, :] < product_count[:, :, None]
    group_ids = jnp.arange(GROUPS, dtype=jnp.int32)

    def one_row(row_id):
        grid_row = row_id // GROUP_ROWS
        partner_rows = group_ids[:, None] * GROUP_ROWS + wanted[row_id]
        summed = jnp.zeros((GROUPS, SLOTS_C, BLOCK, BLOCK), jnp.float32)
        for shift_count in range(STEPS):
            left_group = (group_ids + shift_count) % GROUPS
            left_blocks = blocks[row_id][left_group]
            left_cols = columns[row_id][left_group]
            left_alive = living[row_id][left_group]
            right_group = (grid_row + shift_count) % GROUPS
            right_blocks = blocks[partner_rows, right_group]
            right_cols = columns[partner_rows, right_group]
            right_alive = living[partner_rows, right_group]
            matched = (left_cols[:, None, :, None] == right_cols[:, :, None, :]) & left_alive[:, None, :, None] & right_alive[:, :, None, :]
            chosen = jnp.einsum("vqtk,vqkab->vqtab", matched.astype(jnp.float32), right_blocks, precision=FULL)
            summed = summed + jnp.einsum("vtia,vqtja->vqij", left_blocks, chosen, precision=FULL)
        return jnp.where(kept_slots[row_id][:, :, None, None], summed, 0.0)

    result = lax.map(one_row, jnp.arange(BLOCK_ROWS, dtype=jnp.int32))
    return result.reshape(BLOCK_ROWS, GROUPS * SLOTS_C, BLOCK, BLOCK)
```

```python
import functools

import jax
import jax.numpy as jnp
from jax import lax
from jax.experimental import pallas as pl
from jax.experimental.pallas import tpu as pltpu
from jax.sharding import PartitionSpec as P

WIDTH = 128
ROWS = 8
SLOTS = 3
GROUPS = 32
BLOCKS = ROWS * SLOTS
PARTS = 16
BATCHES = 2
LEFT_PARTS = 4
MESH = pl.DeviceIdType.MESH
HIGH = lax.Precision.HIGHEST


def place(x, y, z_hi, z_lo, core):
    return ((z_lo * 8 + y) * 2 + core, x * 4 + z_hi)


def exchange(far_rows, left_rows, far_src, left_src, far, far_next, left, stage1, stage2,
             s1, r1, s2, r2, s3, r3, s4, r4, s5, r5):
    part = far_rows // PARTS
    size = part // BATCHES
    i, j = lax.axis_index("row"), lax.axis_index("col")
    core, y, z_lo = i % 2, (i // 2) % 8, i // 16
    x, z_hi = j // 4, j % 4
    zh1, zh0 = z_hi // 2, z_hi % 2
    x_top, x_low = x // 4, x % 4
    y_top, y_low = y // 2, y % 2
    flip = lambda bit, by: (bit + by) % 2
    turn2 = z_hi % 2 == core
    turn3 = y_top == x_low

    def hop1(e):
        return place((x + e // 2) % 8, y_top * 2 + flip(y_low, e % 2), z_hi, z_lo, core)

    hop2_groups = [(flip(z_lo, e // 2), flip(zh1, e % 2)) for e in range(4)]
    hop2 = [place(x, y, y0 * 2 + core, x2, zh0) for x2, y0 in hop2_groups]
    hop2_from = [place(x, y, flip(zh1, e % 2) * 2 + core, flip(z_lo, e // 2), zh0) for e in range(4)]
    hop3_slots = [[((y_top + e) % 4, flip(y_low, f % 2), flip(x_top, f // 2)) for e in range(4)] for f in range(4)]
    hop3 = [[place(zl * 4 + y_top, k * 2 + zh, z_hi, z_lo, core) for k, zh, zl in line] for line in hop3_slots]
    hop3_from = [place((x + e // 2) % 8, x_low * 2 + flip(y_low, e % 2), z_hi, z_lo, core) for e in range(PARTS)]
    row_before = ((i + GROUPS - 1) % GROUPS, j)
    row_after = ((i + 1) % GROUPS, j)
    col_before = (i, (j + GROUPS - 1) % GROUPS)
    col_after = (i, (j + 1) % GROUPS)

    barrier = pltpu.get_barrier_semaphore()

    def greet(to):
        pl.semaphore_signal(barrier, inc=1, device_id=to, device_id_type=MESH)

    for e in range(1, PARTS):
        greet(hop1(e))
    for sender in hop2_from + hop3_from:
        greet(sender)
    greet(row_after)
    greet(col_after)
    pl.semaphore_wait(barrier, 2 * (PARTS - 1) + 3 + 2 + 2)

    def remote(src, dst, send_sem, recv_sem, to):
        return pltpu.make_async_remote_copy(
            src_ref=src, dst_ref=dst, send_sem=send_sem, recv_sem=recv_sem, device_id=to, device_id_type=MESH
        )

    sends = []
    turns = []

    def start(*copy):
        made = remote(*copy)
        made.start()
        sends.append(made)

    def start_or_own(own, src, dst, send_sem, recv_sem, to):
        made = remote(src, dst, send_sem, recv_sem, to)

        @pl.when(own)
        def _():
            pltpu.make_async_copy(src, dst, recv_sem).start()

        @pl.when(jnp.logical_not(own))
        def _():
            made.start()

        turns.append((own, made))

    def arrived(ref, sem):
        pltpu.make_async_copy(ref, ref, sem).wait()

    left_size = left_rows // LEFT_PARTS

    def send_left(n):
        span = pl.ds(n * left_size, left_size)
        start(left_src.at[span], left.at[span], s5.at[n], r5.at[n], col_before)

    def rows(at, n=1):
        return pl.ds(pl.multiple_of(at * size, 8), n * size)

    slot1 = (x_top * 2 + y_low) * 4 + x_low
    slot2 = zh1 * 2 + z_lo
    mine = x * 2 + y_low
    for b in range(BATCHES):
        for e in list(range(1, PARTS)) + [0]:
            chunk = ((x + e // 2) % 8) * 2 + flip(y_low, e % 2)
            src = far_src.at[rows(chunk * BATCHES + b)]
            dst = stage1.at[b, rows(slot1)]
            if e:
                start(src, dst, s1.at[b, e], r1.at[b, slot1], hop1(e))
            else:
                pltpu.make_async_copy(src, dst, r1.at[b, slot1]).start()
    for n in range(LEFT_PARTS // 2):
        send_left(n)
    for b in range(BATCHES):
        for e in (1, 2, 3, 0):
            x2, y0 = hop2_groups[e]
            group = x2 * 2 + y0
            for k in range(4):
                arrived(stage1.at[b, rows(group * 4 + k)], r1.at[b, group * 4 + k])
            copy = (stage1.at[b, rows(group * 4, 4)], stage2.at[b, rows(slot2 * 4, 4)], s2.at[b, e], r2.at[b, slot2], hop2[e])
            if e:
                start(*copy)
            else:
                start_or_own(turn2, *copy)
    for b in range(BATCHES):
        for f in (1, 2, 3, 0):
            zh, zl = hop3_slots[f][0][1:]
            slot = zh * 2 + zl
            arrived(stage2.at[b, rows(slot * 4, 4)], r2.at[b, slot])
            for e in (1, 2, 3, 0):
                k = hop3_slots[f][e][0]
                copy = (stage2.at[b, rows(slot * 4 + k)], far.at[rows(mine * BATCHES + b)],
                        s3.at[b, f * 4 + e], r3.at[b, mine], hop3[f][e])
                if e or f:
                    start(*copy)
                else:
                    start_or_own(turn3, *copy)
    for n in range(LEFT_PARTS // 2, LEFT_PARTS):
        send_left(n)
    for b in range(BATCHES):
        for q in range(PARTS):
            span = rows(q * BATCHES + b)
            arrived(far.at[span], r3.at[b, q])
            start(far.at[span], far_next.at[span], s4.at[b, q], r4.at[b, q], row_before)
    for n in range(LEFT_PARTS):
        span = pl.ds(n * left_size, left_size)
        arrived(left.at[span], r5.at[n])
    for b in range(BATCHES):
        for q in range(PARTS):
            span = rows(q * BATCHES + b)
            arrived(far_next.at[span], r4.at[b, q])
    for made in sends:
        made.wait_send()
    for own, made in turns:
        @pl.when(jnp.logical_not(own))
        def _():
            made.wait_send()


def exchanged(far_src, left_src, collective_id):
    far_rows, left_rows = far_src.shape[0], left_src.shape[0]
    shape = lambda rows: jax.ShapeDtypeStruct((rows, WIDTH), jnp.float32)
    anywhere = pl.BlockSpec(memory_space=pl.ANY)
    dma = pltpu.SemaphoreType.DMA
    return pl.pallas_call(
        functools.partial(exchange, far_rows, left_rows),
        out_shape=[shape(far_rows), shape(far_rows), shape(left_rows)],
        in_specs=[anywhere] * 2,
        out_specs=[anywhere] * 3,
        scratch_shapes=[
            pltpu.VMEM((BATCHES, far_rows // BATCHES, WIDTH), jnp.float32),
            pltpu.VMEM((BATCHES, far_rows // BATCHES, WIDTH), jnp.float32),
            dma((BATCHES, PARTS)), dma((BATCHES, PARTS)),
            dma((BATCHES, 4)), dma((BATCHES, 4)),
            dma((BATCHES, PARTS)), dma((BATCHES, PARTS)),
            dma((BATCHES, PARTS)), dma((BATCHES, PARTS)),
            dma((LEFT_PARTS,)), dma((LEFT_PARTS,)),
        ],
        name="exchange",
        compiler_params=pltpu.CompilerParams(
            collective_id=collective_id, has_side_effects=True, vmem_limit_bytes=16 * 1024 * 1024
        ),
    )(far_src, left_src)


def multiply(own, left, far, far_next, panel_cols, panel_count, product_cols, product_count, out,
             left_cols, left_count, right_cols, right_count, want_cols, want_count, sems):
    i, j = lax.axis_index("row"), lax.axis_index("col")
    mine, other = pl.ds(i * ROWS, ROWS), pl.ds(j * ROWS, ROWS)
    copies = [
        pltpu.make_async_copy(table.at[span], to, sems.at[n])
        for n, (table, span, to) in enumerate([
            (panel_cols, mine, left_cols), (panel_count, mine, left_count),
            (panel_cols, other, right_cols), (panel_count, other, right_count),
            (product_cols, mine, want_cols), (product_count, mine, want_count),
        ])
    ]
    for copy in copies:
        copy.start()
    out[...] = jnp.zeros_like(out)
    for copy in copies:
        copy.wait()

    def term(at, a, b):
        out[at] += lax.dot_general(a, b, (((1,), (1,)), ((), ())), precision=HIGH, preferred_element_type=jnp.float32)

    def one_row(r, _):
        def one_slot(q, _):
            c = want_cols[r, j * SLOTS + q]
            for s, (lefts, rights) in enumerate(((own, far), (left, far_next))):
                u, v = (j + s) % GROUPS, (i + s) % GROUPS

                def one_left(t, _):
                    m = left_cols[r, u * SLOTS + t]

                    def one_right(k, _):
                        @pl.when(right_cols[c, v * SLOTS + k] == m)
                        def _():
                            term(r * SLOTS + q, lefts[r * SLOTS + t], rights[c * SLOTS + k])
                        return 0

                    return lax.fori_loop(0, right_count[c, v], one_right, 0)

                lax.fori_loop(0, left_count[r, u], one_left, 0)
            return 0

        return lax.fori_loop(0, want_count[r, j], one_slot, 0)

    lax.fori_loop(0, ROWS, one_row, 0)


def multiplied(own, left, far, far_next, *tables):
    vmem = pl.BlockSpec(memory_space=pltpu.VMEM)
    anywhere = pl.BlockSpec(memory_space=pl.ANY)
    cols, count = pltpu.SMEM((ROWS, GROUPS * SLOTS), jnp.int32), pltpu.SMEM((ROWS, GROUPS), jnp.int32)
    blocks = lambda a: a.reshape(-1, WIDTH, WIDTH)
    return pl.pallas_call(
        multiply,
        out_shape=jax.ShapeDtypeStruct((BLOCKS, WIDTH, WIDTH), jnp.float32),
        in_specs=[vmem] * 4 + [anywhere] * 4,
        out_specs=vmem,
        scratch_shapes=[cols, count] * 3 + [pltpu.SemaphoreType.DMA((6,))],
        name="multiply",
        compiler_params=pltpu.CompilerParams(vmem_limit_bytes=32 * 1024 * 1024),
    )(blocks(own), blocks(left), blocks(far), blocks(far_next), *tables)


def on_device(panel_blocks, panel_cols, panel_count, product_cols, product_count):
    own = panel_blocks.reshape(BLOCKS * WIDTH, WIDTH)
    far, far_next, left = exchanged(own, own, 1)
    product = multiplied(own, left, far, far_next, panel_cols, panel_count, product_cols, product_count)
    return product.reshape(ROWS, SLOTS, WIDTH, WIDTH)


def solution(mesh):
    return jax.shard_map(
        on_device,
        mesh=mesh,
        in_specs=(P("row", "col", None, None), P(), P(), P(), P()),
        out_specs=P("row", "col", None, None),
        check_vma=False,
    )
```

```python
import functools

import jax
import jax.numpy as jnp
from jax import lax
from jax.experimental import pallas as pl
from jax.experimental.pallas import tpu as pltpu
from jax.sharding import PartitionSpec as P

WIDTH = 128
ROWS = 8
SLOTS = 3
GROUPS = 32
BLOCKS = ROWS * SLOTS
PARTS = 16
LEFT_PARTS = 4
LEVELS = ((12, 16, 12), (15, 19, 15))
OWN_COLS, LEFT_COLS, OWN_COUNT, LEFT_COUNT, WANT_COLS, WANT_COUNT = 0, 3, 6, 7, 8, 11
FAR_COLS, NEXT_COLS, FAR_COUNT, NEXT_COUNT, LEFT_OUT, LEFT_IN = 12, 15, 18, 19, 20, 21
FRONT_OUT, REST_OUT, FRONT_IN, REST_IN, TABLE = 24, 32, 40, 48, 56
MESH = pl.DeviceIdType.MESH
HIGH = lax.Precision.HIGHEST


def place(x, y, z_hi, z_lo, core):
    return ((z_lo * 8 + y) * 2 + core, x * 4 + z_hi)


def exchange(far_rows, left_rows, next_rows, batches, far_src, left_src, far, far_next, left, stage1, stage2,
             s1, r1, s2, r2, s3, r3, s4, r4, s5, r5):
    part = far_rows // PARTS
    size = part // batches
    i, j = lax.axis_index("row"), lax.axis_index("col")
    core, y, z_lo = i % 2, (i // 2) % 8, i // 16
    x, z_hi = j // 4, j % 4
    zh1, zh0 = z_hi // 2, z_hi % 2
    x_top, x_low = x // 4, x % 4
    y_top, y_low = y // 2, y % 2
    flip = lambda bit, by: (bit + by) % 2
    turn2 = z_hi % 2 == core
    turn3 = y_top == x_low

    def hop1(e):
        return place((x + e // 2) % 8, y_top * 2 + flip(y_low, e % 2), z_hi, z_lo, core)

    hop2_groups = [(flip(z_lo, e // 2), flip(zh1, e % 2)) for e in range(4)]
    hop2 = [place(x, y, y0 * 2 + core, x2, zh0) for x2, y0 in hop2_groups]
    hop2_from = [place(x, y, flip(zh1, e % 2) * 2 + core, flip(z_lo, e // 2), zh0) for e in range(4)]
    hop3_slots = [[((y_top + e) % 4, flip(y_low, f % 2), flip(x_top, f // 2)) for e in range(4)] for f in range(4)]
    hop3 = [[place(zl * 4 + y_top, k * 2 + zh, z_hi, z_lo, core) for k, zh, zl in line] for line in hop3_slots]
    hop3_from = [place((x + e // 2) % 8, x_low * 2 + flip(y_low, e % 2), z_hi, z_lo, core) for e in range(PARTS)]
    row_before = ((i + GROUPS - 1) % GROUPS, j)
    row_after = ((i + 1) % GROUPS, j)
    col_before = (i, (j + GROUPS - 1) % GROUPS)
    col_after = (i, (j + 1) % GROUPS)

    barrier = pltpu.get_barrier_semaphore()

    def greet(to):
        pl.semaphore_signal(barrier, inc=1, device_id=to, device_id_type=MESH)

    for e in range(1, PARTS):
        greet(hop1(e))
    for sender in hop2_from + hop3_from:
        greet(sender)
    greet(row_after)
    greet(col_after)
    pl.semaphore_wait(barrier, 2 * (PARTS - 1) + 3 + 2 + 2)

    def remote(src, dst, send_sem, recv_sem, to):
        return pltpu.make_async_remote_copy(
            src_ref=src, dst_ref=dst, send_sem=send_sem, recv_sem=recv_sem, device_id=to, device_id_type=MESH
        )

    sends = []
    turns = []

    def start(*copy):
        made = remote(*copy)
        made.start()
        sends.append(made)

    def start_or_own(own, src, dst, send_sem, recv_sem, to):
        made = remote(src, dst, send_sem, recv_sem, to)

        @pl.when(own)
        def _():
            pltpu.make_async_copy(src, dst, recv_sem).start()

        @pl.when(jnp.logical_not(own))
        def _():
            made.start()

        turns.append((own, made))

    def arrived(ref, sem):
        pltpu.make_async_copy(ref, ref, sem).wait()

    left_size = left_rows // LEFT_PARTS

    def send_left(n):
        span = pl.ds(n * left_size, left_size)
        start(left_src.at[span], left.at[span], s5.at[n], r5.at[n], col_before)

    def rows(at, n=1):
        return pl.ds(pl.multiple_of(at * size, 8), n * size)

    slot1 = (x_top * 2 + y_low) * 4 + x_low
    slot2 = zh1 * 2 + z_lo
    mine = x * 2 + y_low
    for b in range(batches):
        for e in list(range(1, PARTS)) + [0]:
            chunk = ((x + e // 2) % 8) * 2 + flip(y_low, e % 2)
            src = far_src.at[rows(chunk * batches + b)]
            dst = stage1.at[b, rows(slot1)]
            if e:
                start(src, dst, s1.at[b, e], r1.at[b, slot1], hop1(e))
            else:
                pltpu.make_async_copy(src, dst, r1.at[b, slot1]).start()
    for n in range(LEFT_PARTS // 2):
        send_left(n)
    for b in range(batches):
        for e in (1, 2, 3, 0):
            x2, y0 = hop2_groups[e]
            group = x2 * 2 + y0
            for k in range(4):
                arrived(stage1.at[b, rows(group * 4 + k)], r1.at[b, group * 4 + k])
            copy = (stage1.at[b, rows(group * 4, 4)], stage2.at[b, rows(slot2 * 4, 4)], s2.at[b, e], r2.at[b, slot2], hop2[e])
            if e:
                start(*copy)
            else:
                start_or_own(turn2, *copy)
    for b in range(batches):
        for f in (1, 2, 3, 0):
            zh, zl = hop3_slots[f][0][1:]
            slot = zh * 2 + zl
            arrived(stage2.at[b, rows(slot * 4, 4)], r2.at[b, slot])
            for e in (1, 2, 3, 0):
                k = hop3_slots[f][e][0]
                copy = (stage2.at[b, rows(slot * 4 + k)], far.at[rows(mine * batches + b)],
                        s3.at[b, f * 4 + e], r3.at[b, mine], hop3[f][e])
                if e or f:
                    start(*copy)
                else:
                    start_or_own(turn3, *copy)
    for n in range(LEFT_PARTS // 2, LEFT_PARTS):
        send_left(n)
    onward = [(b, q) for b in range(batches) for q in range(PARTS)]
    ahead = [(b, q) for b, q in onward if (q * batches + b) * size < next_rows]
    for b, q in ahead + [at for at in onward if at not in ahead]:
        span = rows(q * batches + b)
        arrived(far.at[span], r3.at[b, q])
        if (b, q) in ahead:
            start(far.at[span], far_next.at[span], s4.at[b, q], r4.at[b, q], row_before)
    for n in range(LEFT_PARTS):
        span = pl.ds(n * left_size, left_size)
        arrived(left.at[span], r5.at[n])
    for b, q in ahead:
        arrived(far_next.at[rows(q * batches + b)], r4.at[b, q])
    for made in sends:
        made.wait_send()
    for own, made in turns:
        @pl.when(jnp.logical_not(own))
        def _():
            made.wait_send()


def exchanged(far_src, left_src, far_blocks, left_blocks, next_blocks, batches, collective_id):
    far_rows, left_rows, next_rows = far_blocks * WIDTH, left_blocks * WIDTH, next_blocks * WIDTH
    piece = far_rows // (PARTS * batches)
    next_rows = -(-next_rows // piece) * piece
    shape = lambda rows: jax.ShapeDtypeStruct((rows, WIDTH), jnp.float32)
    anywhere = pl.BlockSpec(memory_space=pl.ANY)
    dma = pltpu.SemaphoreType.DMA
    return pl.pallas_call(
        functools.partial(exchange, far_rows, left_rows, next_rows, batches),
        out_shape=[shape(far_rows), shape(-(-next_rows // WIDTH) * WIDTH), shape(left_rows)],
        in_specs=[anywhere] * 2,
        out_specs=[anywhere] * 3,
        scratch_shapes=[
            pltpu.VMEM((batches, far_rows // batches, WIDTH), jnp.float32),
            pltpu.VMEM((batches, far_rows // batches, WIDTH), jnp.float32),
            dma((batches, PARTS)), dma((batches, PARTS)),
            dma((batches, 4)), dma((batches, 4)),
            dma((batches, PARTS)), dma((batches, PARTS)),
            dma((batches, PARTS)), dma((batches, PARTS)),
            dma((LEFT_PARTS,)), dma((LEFT_PARTS,)),
        ],
        name="exchange",
        compiler_params=pltpu.CompilerParams(
            collective_id=collective_id, has_side_effects=True, vmem_limit_bytes=16 * 1024 * 1024
        ),
    )(far_src, left_src)


def bits_of(cols, count):
    bits = small(1 << cols[...])
    group = lax.broadcasted_iota(jnp.int32, (GROUPS, GROUPS * SLOTS), 0)
    slot = lax.broadcasted_iota(jnp.int32, (GROUPS, GROUPS * SLOTS), 1)
    held = jnp.zeros((GROUPS, ROWS * GROUPS), jnp.int32)
    for t in range(SLOTS):
        bit = whole_dot(small((slot == group * SLOTS + t).astype(jnp.int32)), bits, ((1,), (0,)))
        held = held | jnp.where(count[...] > t, bit.astype(jnp.int32), 0)
    return held


def small(a):
    return a.astype(jnp.float32).astype(jnp.bfloat16)


def whole_dot(a, b, dims):
    return lax.dot_general(a, b, (dims, ((), ())), preferred_element_type=jnp.float32)


def ones_in(mask):
    mask = mask - ((mask >> 1) & 0x55)
    mask = (mask & 0x33) + ((mask >> 2) & 0x33)
    return (mask + (mask >> 4)) & 0x0F


def over_rows(join, a):
    lanes = a.shape[1]
    for step in (4, 2, 1):
        a = join(a, pltpu.roll(a, lanes - step, 1))
    return a


def plan(panel_cols, panel_count, product_cols, product_count, own, level, table, left_src, far_src,
         left_need, front_need, rest_need, numbers, sem):
    lanes = ROWS * GROUPS
    held = bits_of(panel_cols, panel_count)
    asked = bits_of(product_cols, product_count)
    held_next = jnp.concatenate([held[1:], held[:1]], axis=0)
    row = lax.broadcasted_iota(jnp.int32, (lanes, lanes), 0)
    col = lax.broadcasted_iota(jnp.int32, (lanes, lanes), 1)
    pick = ((row % GROUPS) * ROWS + row // GROUPS == col).astype(jnp.float32).astype(jnp.bfloat16)
    turned = small(whole_dot(pick, small(held), ((1,), (1,))))
    group = lax.broadcasted_iota(jnp.int32, (GROUPS, lanes), 0)
    lane = lax.broadcasted_iota(jnp.int32, (GROUPS, lanes), 1)
    widen = lambda s: (group == (lane // ROWS + s) % GROUPS).astype(jnp.float32).astype(jnp.bfloat16)
    right = whole_dot(turned, widen(0), ((1,), (0,))).astype(jnp.int32)
    right_next = whole_dot(turned, widen(1), ((1,), (0,))).astype(jnp.int32)
    left = jnp.zeros_like(held)
    fronts = jnp.zeros_like(held)
    unions = jnp.zeros_like(held)
    either = lambda a, b: a | b
    for w in range(ROWS):
        span = slice(w * GROUPS, (w + 1) * GROUPS)
        chosen = ((asked >> w) & 1) == 1
        left = left | jnp.where(chosen, right_next[span], 0)
        front = over_rows(either, jnp.where(chosen, held_next, 0)) & right_next[span]
        rest = over_rows(either, jnp.where(chosen, held, 0)) & right[span]
        front_need[span, :] = front
        rest_need[span, :] = rest
        fronts += ones_in(front)
        unions += ones_in(rest | pltpu.roll(front, ROWS, 1))
    left = left & held_next
    left_need[...] = left
    first = lane % ROWS == 0
    most = lambda a: jnp.max(jnp.where(first, a, 0))
    most_left, most_front, most_union = most(over_rows(jnp.add, ones_in(left))), most(fronts), most(unions)
    reached = 0
    for left_blocks, far_blocks, next_blocks in LEVELS:
        over = (most_left > left_blocks) | (most_union > far_blocks) | (most_front > next_blocks)
        reached += over.astype(jnp.int32)
    level[0] = reached

    i, j = lax.axis_index("row"), lax.axis_index("col")
    after = lambda n: (n + 1) % GROUPS
    before = lambda n: (n + GROUPS - 1) % GROUPS
    for at, source, start, size in (
        (OWN_COLS, panel_cols, j * SLOTS, SLOTS), (LEFT_COLS, panel_cols, after(j) * SLOTS, SLOTS),
        (OWN_COUNT, panel_count, j, 1), (LEFT_COUNT, panel_count, after(j), 1),
        (WANT_COLS, product_cols, j * SLOTS, SLOTS), (WANT_COUNT, product_count, j, 1),
        (FAR_COLS, panel_cols, i * SLOTS, SLOTS), (NEXT_COLS, panel_cols, after(i) * SLOTS, SLOTS),
        (FAR_COUNT, panel_count, i, 1), (NEXT_COUNT, panel_count, after(i), 1),
        (LEFT_OUT, left_need, before(j), 1), (LEFT_IN, left_need, j, 1),
    ):
        for n in range(size):
            table[pl.ds(at + n, 1), :] = source[pl.ds(start + n, 1), :]
    for at, source, start in (
        (FRONT_OUT, front_need, i), (REST_OUT, rest_need, i), (FRONT_IN, front_need, j), (REST_IN, rest_need, j),
    ):
        for w in range(ROWS):
            table[pl.ds(at + w, 1), :] = source[pl.ds(start + w * GROUPS, 1), :]
    copy = pltpu.make_async_copy(table, numbers, sem)
    copy.start()
    copy.wait()

    mine = i * ROWS

    def pack(needed, to, at):
        def one_row(r, at):
            for t in range(SLOTS):
                take = (numbers[OWN_COUNT, mine + r] > t) & (((needed(r) >> numbers[OWN_COLS + t, mine + r]) & 1) == 1)

                @pl.when(take & (at < to.shape[0]))
                def _():
                    to[at] = own[r * SLOTS + t]

                at = at + take.astype(jnp.int32)
            return at

        return lax.fori_loop(0, ROWS, one_row, at)

    front = lambda r: numbers[FRONT_OUT + r, before(j) * ROWS]
    pack(lambda r: numbers[LEFT_OUT, mine + r], left_src, 0)
    pack(lambda r: numbers[REST_OUT + r, j * ROWS] & ~front(r), far_src, pack(front, far_src, 0))


def planned(own, *tables):
    vmem = pl.BlockSpec(memory_space=pltpu.VMEM)
    block = lambda n: jax.ShapeDtypeStruct((n, WIDTH, WIDTH), jnp.float32)
    numbers = (TABLE, ROWS * GROUPS)
    need = pltpu.VMEM((ROWS * GROUPS, ROWS * GROUPS), jnp.int32)
    return pl.pallas_call(
        plan,
        out_shape=[
            jax.ShapeDtypeStruct((1,), jnp.int32), jax.ShapeDtypeStruct(numbers, jnp.int32),
            block(LEVELS[-1][0]), block(LEVELS[-1][1]),
        ],
        in_specs=[vmem] * 5,
        out_specs=[pl.BlockSpec(memory_space=pltpu.SMEM), vmem, vmem, vmem],
        scratch_shapes=[
            pltpu.VMEM((GROUPS, ROWS * GROUPS), jnp.int32), need, need,
            pltpu.SMEM(numbers, jnp.int32), pltpu.SemaphoreType.DMA,
        ],
        name="plan",
        compiler_params=pltpu.CompilerParams(vmem_limit_bytes=32 * 1024 * 1024),
    )(*tables, own)


def multiply(packed, table, own, left, far, far_next, out, places):
    i, j = lax.axis_index("row"), lax.axis_index("col")
    mine, other = i * ROWS, j * ROWS
    out[...] = jnp.zeros_like(out)

    def number(which, count, cols, base, needed, at):
        def one_row(r, at):
            for t in range(SLOTS):
                take = (table[count, base + r] > t) & (((needed(r) >> table[cols + t, base + r]) & 1) == 1)

                @pl.when(take)
                def _():
                    places[which, r * SLOTS + t] = at

                at = at + take.astype(jnp.int32)
            return at

        return lax.fori_loop(0, ROWS, one_row, at)

    if packed:
        front = lambda w: table[FRONT_IN + w, ((i + GROUPS - 1) % GROUPS) * ROWS]
        number(0, LEFT_COUNT, LEFT_COLS, mine, lambda r: table[LEFT_IN, mine + r], 0)
        number(2, NEXT_COUNT, NEXT_COLS, other, lambda w: table[FRONT_IN + w, mine], 0)
        size = number(1, FAR_COUNT, FAR_COLS, other, front, 0)
        number(1, FAR_COUNT, FAR_COLS, other, lambda w: table[REST_IN + w, mine] & ~front(w), size)
    place_of = lambda which, slot: places[which, slot] if packed else slot

    def term(at, a, b):
        out[at] += lax.dot_general(a, b, (((1,), (1,)), ((), ())), precision=HIGH, preferred_element_type=jnp.float32)

    sides = (
        (OWN_COUNT, OWN_COLS, own, lambda slot: slot, FAR_COUNT, FAR_COLS, far, lambda slot: place_of(1, slot)),
        (LEFT_COUNT, LEFT_COLS, left, lambda slot: place_of(0, slot), NEXT_COUNT, NEXT_COLS, far_next,
         lambda slot: place_of(2, slot)),
    )

    def one_row(r, _):
        def one_slot(q, _):
            c = table[WANT_COLS + q, mine + r]
            for left_count, left_cols, lefts, left_at, right_count, right_cols, rights, right_at in sides:
                def one_left(t, _):
                    m = table[left_cols + t, mine + r]

                    def one_right(k, _):
                        @pl.when(table[right_cols + k, other + c] == m)
                        def _():
                            term(r * SLOTS + q, lefts[left_at(r * SLOTS + t)], rights[right_at(c * SLOTS + k)])
                        return 0

                    return lax.fori_loop(0, table[right_count, other + c], one_right, 0)

                lax.fori_loop(0, table[left_count, mine + r], one_left, 0)
            return 0

        return lax.fori_loop(0, table[WANT_COUNT, mine + r], one_slot, 0)

    lax.fori_loop(0, ROWS, one_row, 0)


def multiplied(packed, table, *arrays):
    vmem = pl.BlockSpec(memory_space=pltpu.VMEM)
    return pl.pallas_call(
        functools.partial(multiply, packed),
        out_shape=jax.ShapeDtypeStruct((BLOCKS, WIDTH, WIDTH), jnp.float32),
        in_specs=[pl.BlockSpec(memory_space=pltpu.SMEM)] + [vmem] * 4,
        out_specs=vmem,
        scratch_shapes=[pltpu.SMEM((3, BLOCKS), jnp.int32)],
        name="multiply",
        compiler_params=pltpu.CompilerParams(vmem_limit_bytes=32 * 1024 * 1024),
    )(table, *(a.reshape(-1, WIDTH, WIDTH) for a in arrays))


def on_device(panel_blocks, panel_cols, panel_count, product_cols, product_count):
    own = panel_blocks.reshape(BLOCKS, WIDTH, WIDTH)
    flat = lambda a: a.reshape(-1, WIDTH)
    level, table, left_src, far_src = planned(own, panel_cols.T, panel_count.T, product_cols.T, product_count.T)

    def at_level(n):
        def run():
            if n < len(LEVELS):
                left_blocks, far_blocks, next_blocks = LEVELS[n]
                sent = exchanged(flat(far_src), flat(left_src), far_blocks, left_blocks, next_blocks, 1, n + 1)
            else:
                sent = exchanged(flat(own), flat(own), BLOCKS, BLOCKS, BLOCKS, 2, n + 1)
            far, far_next, left = sent
            return multiplied(n < len(LEVELS), table, own, left, far, far_next)
        return run

    product = lax.switch(level[0], [at_level(n) for n in range(len(LEVELS) + 1)])
    return product.reshape(ROWS, SLOTS, WIDTH, WIDTH)


def solution(mesh):
    return jax.shard_map(
        on_device,
        mesh=mesh,
        in_specs=(P("row", "col", None, None), P(), P(), P(), P()),
        out_specs=P("row", "col", None, None),
        check_vma=False,
    )
```

```python
import functools

import jax
import jax.numpy as jnp
from jax import lax
from jax.experimental import pallas as pl
from jax.experimental.pallas import tpu as pltpu
from jax.sharding import PartitionSpec as P

WIDTH = 128
ROWS = 8
SLOTS = 3
GROUPS = 32
BLOCKS = ROWS * SLOTS
PARTS = 16
LEFT_PARTS = 4
AHEAD = 2
LEFT_FIRST = 1
LEFT_EARLY = 1
LEVELS = ((12, 16, 12, 2), (14, 18, 14, 2))
OWN_COLS, LEFT_COLS, OWN_COUNT, LEFT_COUNT, WANT_COLS, WANT_COUNT = 0, 3, 6, 7, 8, 11
FAR_COLS, NEXT_COLS, FAR_COUNT, NEXT_COUNT, LEFT_OUT, LEFT_IN = 12, 15, 18, 19, 20, 21
FRONT_OUT, REST_OUT, FRONT_IN, REST_IN, TABLE = 24, 32, 40, 48, 56
MESH = pl.DeviceIdType.MESH


def place(x, y, z_hi, z_lo, core):
    return ((z_lo * 8 + y) * 2 + core, x * 4 + z_hi)


def exchange(far_rows, left_rows, next_rows, batches, far_src, left_src, far, far_next, left, stage1, stage2, stage3,
             s1, r1, s2, r2, s3, r3, s6, r6, s4, r4, s5, r5):
    part = far_rows // PARTS
    size = part // batches
    i, j = lax.axis_index("row"), lax.axis_index("col")
    core, y, z_lo = i % 2, (i // 2) % 8, i // 16
    x, z_hi = j // 4, j % 4
    zh1, zh0 = z_hi // 2, z_hi % 2
    x_top, x_low = x // 4, x % 4
    y_top, y_low = y // 2, y % 2
    flip = lambda bit, by: (bit + by) % 2
    turn2 = z_hi % 2 == core

    def hop1(e):
        return place((x + e // 2) % 8, y_top * 2 + flip(y_low, e % 2), z_hi, z_lo, core)

    hop2_groups = [(flip(z_lo, e // 2), flip(zh1, e % 2)) for e in range(4)]
    hop2 = [place(x, y, y0 * 2 + core, x2, zh0) for x2, y0 in hop2_groups]
    hop2_from = [place(x, y, flip(zh1, e % 2) * 2 + core, flip(z_lo, e // 2), zh0) for e in range(4)]
    along_y = lambda d: place(x, (y + d) % 8, z_hi, z_lo, core)
    along_x = lambda d: place((x + d) % 8, y, z_hi, z_lo, core)
    row_before = ((i + GROUPS - 1) % GROUPS, j)
    row_after = ((i + 1) % GROUPS, j)
    col_before = (i, (j + GROUPS - 1) % GROUPS)
    col_after = (i, (j + 1) % GROUPS)

    barrier = pltpu.get_barrier_semaphore()

    def greet(to):
        pl.semaphore_signal(barrier, inc=1, device_id=to, device_id_type=MESH)

    for e in range(1, PARTS):
        greet(hop1(e))
    for sender in hop2_from:
        greet(sender)
    for d in range(1, 8):
        greet(along_y(d))
        greet(along_x(d))
    greet(row_after)
    greet(col_after)
    pl.semaphore_wait(barrier, PARTS - 1 + 4 + 7 + 7 + 2)

    def remote(src, dst, send_sem, recv_sem, to):
        return pltpu.make_async_remote_copy(
            src_ref=src, dst_ref=dst, send_sem=send_sem, recv_sem=recv_sem, device_id=to, device_id_type=MESH
        )

    sends = []
    turns = []

    def start(*copy):
        made = remote(*copy)
        made.start()
        sends.append(made)

    def start_or_own(own, src, dst, send_sem, recv_sem, to):
        made = remote(src, dst, send_sem, recv_sem, to)

        @pl.when(own)
        def _():
            pltpu.make_async_copy(src, dst, recv_sem).start()

        @pl.when(jnp.logical_not(own))
        def _():
            made.start()

        turns.append((own, made))

    def arrived(ref, sem):
        pltpu.make_async_copy(ref, ref, sem).wait()

    left_size = left_rows // LEFT_PARTS

    def send_left(n):
        span = pl.ds(n * left_size, left_size)
        start(left_src.at[span], left.at[span], s5.at[n], r5.at[n], col_before)

    def rows(at, n=1):
        return pl.ds(pl.multiple_of(at * size, 8), n * size)

    slot1 = (x_top * 2 + y_low) * 4 + x_low
    slot2 = zh1 * 2 + z_lo

    def spread(b):
        for e in list(range(1, PARTS)) + [0]:
            chunk = ((x + e // 2) % 8) * 2 + flip(y_low, e % 2)
            src, dst, sem = far_src.at[rows(b * PARTS + chunk)], stage1.at[b, rows(slot1)], r1.at[b, slot1]
            if e:
                start(src, dst, s1.at[b, e], sem, hop1(e))
            else:
                pltpu.make_async_copy(src, dst, sem).start()

    def turn_z(b):
        for e in (1, 2, 3, 0):
            x2, y0 = hop2_groups[e]
            group = x2 * 2 + y0
            for k in range(4):
                arrived(stage1.at[b, rows(group * 4 + k)], r1.at[b, group * 4 + k])
            copy = (stage1.at[b, rows(group * 4, 4)], stage2.at[b, rows(slot2 * 4, 4)], s2.at[b, e], r2.at[b, slot2], hop2[e])
            if e:
                start(*copy)
            else:
                start_or_own(turn2, *copy)

    def turn_y(b):
        for slot in range(4):
            arrived(stage2.at[b, rows(slot * 4, 4)], r2.at[b, slot])
        for d in (4, 3, 5, 2, 6, 1, 7, 0):
            to = (y + d) % 8
            for zl in range(2):
                src = stage2.at[b, rows((to % 2 * 2 + zl) * 4 + to // 2)]
                at = (zl * 4 + y_top) * 2 + y_low
                dst, sem = stage3.at[b, rows(at)], r3.at[b, at]
                if d:
                    start(src, dst, s3.at[b, d, zl], sem, along_y(d))
                else:
                    pltpu.make_async_copy(src, dst, sem).start()

    def turn_x(b):
        for d in (4, 3, 5, 2, 6, 1, 7, 0):
            to = (x + d) % 8
            for k in range(2):
                arrived(stage3.at[b, rows(to * 2 + k)], r3.at[b, to * 2 + k])
            src, dst, sem = stage3.at[b, rows(to * 2, 2)], far.at[rows(b * PARTS + x * 2, 2)], r6.at[b, x]
            if d:
                start(src, dst, s6.at[b, d], sem, along_x(d))
            else:
                pltpu.make_async_copy(src, dst, sem).start()

    pairs = [rows(b * PARTS + 2 * q, 2) for b in range(batches) for q in range(8)]

    def ahead(b, q):
        return (b * PARTS + 2 * q) * size < next_rows

    def hand_on(b):
        for q in range(8):
            span = pairs[b * 8 + q]
            arrived(far.at[span], r6.at[b, q])
            if ahead(b, q):
                start(far.at[span], far_next.at[span], s4.at[b, q], r4.at[b, q], row_before)

    lefts = list(range(LEFT_PARTS))
    for b in range(min(AHEAD, batches)):
        spread(b)
    for _ in range(LEFT_FIRST):
        send_left(lefts.pop(0))
    for step in range(batches + 3):
        if step < batches:
            turn_z(step)
            if step + AHEAD < batches:
                spread(step + AHEAD)
        if step >= batches - LEFT_EARLY:
            while lefts:
                send_left(lefts.pop(0))
        if 0 <= step - 1 < batches:
            turn_y(step - 1)
        if 0 <= step - 2 < batches:
            turn_x(step - 2)
        if 0 <= step - 3 < batches:
            hand_on(step - 3)
    for n in range(LEFT_PARTS):
        span = pl.ds(n * left_size, left_size)
        arrived(left.at[span], r5.at[n])
    for b in range(batches):
        for q in range(8):
            if ahead(b, q):
                arrived(far_next.at[pairs[b * 8 + q]], r4.at[b, q])
    for made in sends:
        made.wait_send()
    for own, made in turns:
        @pl.when(jnp.logical_not(own))
        def _():
            made.wait_send()


def exchanged(far_src, left_src, far_blocks, left_blocks, next_blocks, batches, collective_id):
    far_rows, left_rows, next_rows = far_blocks * WIDTH, left_blocks * WIDTH, next_blocks * WIDTH
    piece = 2 * far_rows // (PARTS * batches)
    next_rows = -(-next_rows // piece) * piece
    shape = lambda rows: jax.ShapeDtypeStruct((rows, WIDTH), jnp.float32)
    anywhere = pl.BlockSpec(memory_space=pl.ANY)
    dma = pltpu.SemaphoreType.DMA
    return pl.pallas_call(
        functools.partial(exchange, far_rows, left_rows, next_rows, batches),
        out_shape=[shape(far_rows), shape(-(-next_rows // WIDTH) * WIDTH), shape(left_rows)],
        in_specs=[anywhere] * 2,
        out_specs=[anywhere] * 3,
        scratch_shapes=[
            pltpu.VMEM((batches, far_rows // batches, WIDTH), jnp.float32),
            pltpu.VMEM((batches, far_rows // batches, WIDTH), jnp.float32),
            pltpu.VMEM((batches, far_rows // batches, WIDTH), jnp.float32),
            dma((batches, PARTS)), dma((batches, PARTS)),
            dma((batches, 4)), dma((batches, 4)),
            dma((batches, 8, 2)), dma((batches, PARTS)),
            dma((batches, 8)), dma((batches, 8)),
            dma((batches, 8)), dma((batches, 8)),
            dma((LEFT_PARTS,)), dma((LEFT_PARTS,)),
        ],
        name="exchange",
        compiler_params=pltpu.CompilerParams(
            collective_id=collective_id, has_side_effects=True, vmem_limit_bytes=16 * 1024 * 1024
        ),
    )(far_src, left_src)


def bits_of(cols, count):
    bits = small(1 << cols[...])
    group = lax.broadcasted_iota(jnp.int32, (GROUPS, GROUPS * SLOTS), 0)
    slot = lax.broadcasted_iota(jnp.int32, (GROUPS, GROUPS * SLOTS), 1)
    held = jnp.zeros((GROUPS, ROWS * GROUPS), jnp.int32)
    for t in range(SLOTS):
        bit = whole_dot(small((slot == group * SLOTS + t).astype(jnp.int32)), bits, ((1,), (0,)))
        held = held | jnp.where(count[...] > t, bit.astype(jnp.int32), 0)
    return held


def small(a):
    return a.astype(jnp.float32).astype(jnp.bfloat16)


def whole_dot(a, b, dims):
    return lax.dot_general(a, b, (dims, ((), ())), preferred_element_type=jnp.float32)


def ones_in(mask):
    mask = mask - ((mask >> 1) & 0x55)
    mask = (mask & 0x33) + ((mask >> 2) & 0x33)
    return (mask + (mask >> 4)) & 0x0F


def over_rows(join, a):
    lanes = a.shape[1]
    for step in (4, 2, 1):
        a = join(a, pltpu.roll(a, lanes - step, 1))
    return a


def plan(panel_cols, panel_count, product_cols, product_count, own, level, table, left_src, far_src,
         left_need, front_need, rest_need, numbers, sem):
    lanes = ROWS * GROUPS
    held = bits_of(panel_cols, panel_count)
    asked = bits_of(product_cols, product_count)
    held_next = jnp.concatenate([held[1:], held[:1]], axis=0)
    row = lax.broadcasted_iota(jnp.int32, (lanes, lanes), 0)
    col = lax.broadcasted_iota(jnp.int32, (lanes, lanes), 1)
    pick = ((row % GROUPS) * ROWS + row // GROUPS == col).astype(jnp.float32).astype(jnp.bfloat16)
    turned = small(whole_dot(pick, small(held), ((1,), (1,))))
    group = lax.broadcasted_iota(jnp.int32, (GROUPS, lanes), 0)
    lane = lax.broadcasted_iota(jnp.int32, (GROUPS, lanes), 1)
    widen = lambda s: (group == (lane // ROWS + s) % GROUPS).astype(jnp.float32).astype(jnp.bfloat16)
    right = whole_dot(turned, widen(0), ((1,), (0,))).astype(jnp.int32)
    right_next = whole_dot(turned, widen(1), ((1,), (0,))).astype(jnp.int32)
    left = jnp.zeros_like(held)
    fronts = jnp.zeros_like(held)
    unions = jnp.zeros_like(held)
    either = lambda a, b: a | b
    for w in range(ROWS):
        span = slice(w * GROUPS, (w + 1) * GROUPS)
        chosen = ((asked >> w) & 1) == 1
        left = left | jnp.where(chosen, right_next[span], 0)
        front = over_rows(either, jnp.where(chosen, held_next, 0)) & right_next[span]
        rest = over_rows(either, jnp.where(chosen, held, 0)) & right[span]
        front_need[span, :] = front
        rest_need[span, :] = rest
        fronts += ones_in(front)
        unions += ones_in(rest | pltpu.roll(front, ROWS, 1))
    left = left & held_next
    left_need[...] = left
    first = lane % ROWS == 0
    most = lambda a: jnp.max(jnp.where(first, a, 0))
    most_left, most_front, most_union = most(over_rows(jnp.add, ones_in(left))), most(fronts), most(unions)
    reached = 0
    for left_blocks, far_blocks, next_blocks, _ in LEVELS:
        over = (most_left > left_blocks) | (most_union > far_blocks) | (most_front > next_blocks)
        reached += over.astype(jnp.int32)
    level[0] = reached

    i, j = lax.axis_index("row"), lax.axis_index("col")
    after = lambda n: (n + 1) % GROUPS
    before = lambda n: (n + GROUPS - 1) % GROUPS
    for at, source, start, size in (
        (OWN_COLS, panel_cols, j * SLOTS, SLOTS), (LEFT_COLS, panel_cols, after(j) * SLOTS, SLOTS),
        (OWN_COUNT, panel_count, j, 1), (LEFT_COUNT, panel_count, after(j), 1),
        (WANT_COLS, product_cols, j * SLOTS, SLOTS), (WANT_COUNT, product_count, j, 1),
        (FAR_COLS, panel_cols, i * SLOTS, SLOTS), (NEXT_COLS, panel_cols, after(i) * SLOTS, SLOTS),
        (FAR_COUNT, panel_count, i, 1), (NEXT_COUNT, panel_count, after(i), 1),
        (LEFT_OUT, left_need, before(j), 1), (LEFT_IN, left_need, j, 1),
    ):
        for n in range(size):
            table[pl.ds(at + n, 1), :] = source[pl.ds(start + n, 1), :]
    for at, source, start in (
        (FRONT_OUT, front_need, i), (REST_OUT, rest_need, i), (FRONT_IN, front_need, j), (REST_IN, rest_need, j),
    ):
        for w in range(ROWS):
            table[pl.ds(at + w, 1), :] = source[pl.ds(start + w * GROUPS, 1), :]
    copy = pltpu.make_async_copy(table, numbers, sem)
    copy.start()
    copy.wait()

    mine = i * ROWS

    def pack(needed, to, at):
        def one_row(r, at):
            for t in range(SLOTS):
                take = (numbers[OWN_COUNT, mine + r] > t) & (((needed(r) >> numbers[OWN_COLS + t, mine + r]) & 1) == 1)

                @pl.when(take & (at < to.shape[0]))
                def _():
                    to[at] = own[r * SLOTS + t]

                at = at + take.astype(jnp.int32)
            return at

        return lax.fori_loop(0, ROWS, one_row, at)

    front = lambda r: numbers[FRONT_OUT + r, before(j) * ROWS]
    pack(lambda r: numbers[LEFT_OUT, mine + r], left_src, 0)
    pack(lambda r: numbers[REST_OUT + r, j * ROWS] & ~front(r), far_src, pack(front, far_src, 0))


def planned(own, *tables):
    vmem = pl.BlockSpec(memory_space=pltpu.VMEM)
    block = lambda n: jax.ShapeDtypeStruct((n, WIDTH, WIDTH), jnp.float32)
    numbers = (TABLE, ROWS * GROUPS)
    need = pltpu.VMEM((ROWS * GROUPS, ROWS * GROUPS), jnp.int32)
    return pl.pallas_call(
        plan,
        out_shape=[
            jax.ShapeDtypeStruct((1,), jnp.int32), jax.ShapeDtypeStruct(numbers, jnp.int32),
            block(LEVELS[-1][0]), block(LEVELS[-1][1]),
        ],
        in_specs=[vmem] * 5,
        out_specs=[pl.BlockSpec(memory_space=pltpu.SMEM), vmem, vmem, vmem],
        scratch_shapes=[
            pltpu.VMEM((GROUPS, ROWS * GROUPS), jnp.int32), need, need,
            pltpu.SMEM(numbers, jnp.int32), pltpu.SemaphoreType.DMA,
        ],
        name="plan",
        compiler_params=pltpu.CompilerParams(vmem_limit_bytes=32 * 1024 * 1024),
    )(*tables, own)


def multiply(packed, table, own, left, far, far_next, out, places):
    i, j = lax.axis_index("row"), lax.axis_index("col")
    mine, other = i * ROWS, j * ROWS
    out[...] = jnp.zeros_like(out)

    def number(which, count, cols, base, needed, at):
        def one_row(r, at):
            for t in range(SLOTS):
                take = (table[count, base + r] > t) & (((needed(r) >> table[cols + t, base + r]) & 1) == 1)

                @pl.when(take)
                def _():
                    places[which, r * SLOTS + t] = at

                at = at + take.astype(jnp.int32)
            return at

        return lax.fori_loop(0, ROWS, one_row, at)

    if packed:
        front = lambda w: table[FRONT_IN + w, ((i + GROUPS - 1) % GROUPS) * ROWS]
        number(0, LEFT_COUNT, LEFT_COLS, mine, lambda r: table[LEFT_IN, mine + r], 0)
        number(2, NEXT_COUNT, NEXT_COLS, other, lambda w: table[FRONT_IN + w, mine], 0)
        size = number(1, FAR_COUNT, FAR_COLS, other, front, 0)
        number(1, FAR_COUNT, FAR_COLS, other, lambda w: table[REST_IN + w, mine] & ~front(w), size)
    place_of = lambda which, slot: places[which, slot] if packed else slot

    def halves(a):
        high = a.astype(jnp.bfloat16)
        return high, (a - high.astype(jnp.float32)).astype(jnp.bfloat16)

    def term(at, a, b):
        (a_high, a_low), (b_high, b_low) = halves(a), halves(b)
        dot = lambda p, q: whole_dot(p, q, ((1,), (1,)))
        out[at] += dot(a_high, b_high) + (dot(a_high, b_low) + dot(a_low, b_high))

    sides = (
        (OWN_COUNT, OWN_COLS, own, lambda slot: slot, FAR_COUNT, FAR_COLS, far, lambda slot: place_of(1, slot)),
        (LEFT_COUNT, LEFT_COLS, left, lambda slot: place_of(0, slot), NEXT_COUNT, NEXT_COLS, far_next,
         lambda slot: place_of(2, slot)),
    )

    def one_row(r, _):
        def one_slot(q, _):
            c = table[WANT_COLS + q, mine + r]
            for left_count, left_cols, lefts, left_at, right_count, right_cols, rights, right_at in sides:
                def one_left(t, _):
                    m = table[left_cols + t, mine + r]

                    def one_right(k, _):
                        @pl.when(table[right_cols + k, other + c] == m)
                        def _():
                            term(r * SLOTS + q, lefts[left_at(r * SLOTS + t)], rights[right_at(c * SLOTS + k)])
                        return 0

                    return lax.fori_loop(0, table[right_count, other + c], one_right, 0)

                lax.fori_loop(0, table[left_count, mine + r], one_left, 0)
            return 0

        return lax.fori_loop(0, table[WANT_COUNT, mine + r], one_slot, 0)

    lax.fori_loop(0, ROWS, one_row, 0)


def multiplied(packed, table, *arrays):
    vmem = pl.BlockSpec(memory_space=pltpu.VMEM)
    return pl.pallas_call(
        functools.partial(multiply, packed),
        out_shape=jax.ShapeDtypeStruct((BLOCKS, WIDTH, WIDTH), jnp.float32),
        in_specs=[pl.BlockSpec(memory_space=pltpu.SMEM)] + [vmem] * 4,
        out_specs=vmem,
        scratch_shapes=[pltpu.SMEM((3, BLOCKS), jnp.int32)],
        name="multiply",
        compiler_params=pltpu.CompilerParams(vmem_limit_bytes=32 * 1024 * 1024),
    )(table, *(a.reshape(-1, WIDTH, WIDTH) for a in arrays))


def on_device(panel_blocks, panel_cols, panel_count, product_cols, product_count):
    own = panel_blocks.reshape(BLOCKS, WIDTH, WIDTH)
    flat = lambda a: a.reshape(-1, WIDTH)
    level, table, left_src, far_src = planned(own, panel_cols.T, panel_count.T, product_cols.T, product_count.T)

    def at_level(n):
        def run():
            if n < len(LEVELS):
                left_blocks, far_blocks, next_blocks, batches = LEVELS[n]
                sent = exchanged(flat(far_src), flat(left_src), far_blocks, left_blocks, next_blocks, batches, n + 1)
            else:
                sent = exchanged(flat(own), flat(own), BLOCKS, BLOCKS, BLOCKS, 1, n + 1)
            far, far_next, left = sent
            return multiplied(n < len(LEVELS), table, own, left, far, far_next)
        return run

    product = lax.switch(level[0], [at_level(n) for n in range(len(LEVELS) + 1)])
    return product.reshape(ROWS, SLOTS, WIDTH, WIDTH)


def solution(mesh):
    return jax.shard_map(
        on_device,
        mesh=mesh,
        in_specs=(P("row", "col", None, None), P(), P(), P(), P()),
        out_specs=P("row", "col", None, None),
        check_vma=False,
    )
```

```python
import functools

import jax
import jax.numpy as jnp
from jax import lax
from jax.experimental import pallas as pl
from jax.experimental.pallas import tpu as pltpu
from jax.sharding import PartitionSpec as P

WIDTH = 128
ROWS = 8
SLOTS = 3
GROUPS = 32
BLOCKS = ROWS * SLOTS
PARTS = 16
LEFT_PARTS = 4
LEFT_FIRST = 1
LEVELS = ((12, 16, 12), (14, 18, 14))
OWN_COLS, LEFT_COLS, OWN_COUNT, LEFT_COUNT, WANT_COLS, WANT_COUNT = 0, 3, 6, 7, 8, 11
FAR_COLS, NEXT_COLS, FAR_COUNT, NEXT_COUNT, LEFT_OUT, LEFT_IN = 12, 15, 18, 19, 20, 21
FRONT_OUT, REST_OUT, FRONT_IN, REST_IN, TABLE = 24, 32, 40, 48, 56
MESH = pl.DeviceIdType.MESH


def place(x, y, z_hi, z_lo, core):
    return ((z_lo * 8 + y) * 2 + core, x * 4 + z_hi)


def exchange(far_rows, left_rows, next_rows, far_src, left_src, far, far_next, left, stage0, stage1, stage2, stage3,
             s0, r0, s1, r1, s2, r2, s3, r3, s4, r4, s5, r5, s6, r6, s7, s8, r8):
    size = far_rows // (2 * PARTS)
    i, j = lax.axis_index("row"), lax.axis_index("col")
    core, y, z_lo = i % 2, (i // 2) % 8, i // 16
    x, z_hi = j // 4, j % 4
    zh1, zh0 = z_hi // 2, z_hi % 2
    x_top, x_low = x // 4, x % 4
    y_top, y_low = y // 2, y % 2
    flip = lambda bit, by: (bit + by) % 2
    turn2 = z_hi % 2 == core

    def hop1(e):
        return place((x + e // 2) % 8, y_top * 2 + flip(y_low, e % 2), z_hi, z_lo, core)

    def hop1_y(e):
        return place(x, (y + e // 2) % 8, z_hi, flip(z_lo, e % 2), core)

    hop2_groups = [(flip(z_lo, e // 2), flip(zh1, e % 2)) for e in range(4)]
    hop2 = [place(x, y, y0 * 2 + core, x2, zh0) for x2, y0 in hop2_groups]
    hop2_from = [place(x, y, flip(zh1, e % 2) * 2 + core, flip(z_lo, e // 2), zh0) for e in range(4)]
    along_y = lambda d: place(x, (y + d) % 8, z_hi, z_lo, core)
    along_x = lambda d: place((x + d) % 8, y, z_hi, z_lo, core)
    row_before = ((i + GROUPS - 1) % GROUPS, j)
    row_after = ((i + 1) % GROUPS, j)
    col_before = (i, (j + GROUPS - 1) % GROUPS)
    col_after = (i, (j + 1) % GROUPS)

    barrier = pltpu.get_barrier_semaphore()

    def greet(to):
        pl.semaphore_signal(barrier, inc=1, device_id=to, device_id_type=MESH)

    for e in range(1, PARTS):
        greet(hop1(e))
        greet(hop1_y(e))
    for sender in hop2_from:
        greet(sender)
    greet(row_after)
    greet(col_after)
    pl.semaphore_wait(barrier, 2 * (PARTS - 1) + 4 + 2)

    def remote(src, dst, send_sem, recv_sem, to):
        return pltpu.make_async_remote_copy(
            src_ref=src, dst_ref=dst, send_sem=send_sem, recv_sem=recv_sem, device_id=to, device_id_type=MESH
        )

    sends = []
    turns = []

    def start(*copy):
        made = remote(*copy)
        made.start()
        sends.append(made)

    def start_or_own(own, src, dst, send_sem, recv_sem, to):
        made = remote(src, dst, send_sem, recv_sem, to)

        @pl.when(own)
        def _():
            pltpu.make_async_copy(src, dst, recv_sem).start()

        @pl.when(jnp.logical_not(own))
        def _():
            made.start()

        turns.append((own, made))

    def arrived(ref, sem):
        pltpu.make_async_copy(ref, ref, sem).wait()

    left_size = left_rows // LEFT_PARTS

    def send_left(n):
        span = pl.ds(n * left_size, left_size)
        start(left_src.at[span], left.at[span], s5.at[n], r5.at[n], col_before)

    def rows(at, n=1):
        return pl.ds(pl.multiple_of(at * size, 8), n * size)

    slot2 = zh1 * 2 + z_lo
    far_first = (4, 3, 5, 2, 6, 1, 7, 0)

    def start_or_copy(d, src, dst, send_sem, recv_sem, to):
        if d:
            start(src, dst, send_sem, recv_sem, to)
        else:
            pltpu.make_async_copy(src, dst, recv_sem).start()

    def spread_y():
        at = (z_lo * 4 + y_top) * 2 + y_low
        for e in list(range(1, PARTS)) + [0]:
            chunk = ((y + e // 2) % 8) * 2 + flip(z_lo, e % 2)
            start_or_copy(e, far_src.at[rows(chunk)], stage0.at[rows(at)], s0.at[e], r0.at[at], hop1_y(e))

    def spread_x():
        at = (x_top * 2 + y_low) * 4 + x_low
        for e in list(range(1, PARTS)) + [0]:
            chunk = PARTS + ((x + e // 2) % 8) * 2 + flip(y_low, e % 2)
            start_or_copy(e, far_src.at[rows(chunk)], stage1.at[1, rows(at)], s1.at[e], r1.at[1, at], hop1(e))

    def cross_x():
        for d in far_first:
            to = (x + d) % 8
            for k in range(2):
                arrived(stage0.at[rows(to * 2 + k)], r0.at[to * 2 + k])
                at = (x_top * 2 + k) * 4 + x_low
                start_or_copy(d, stage0.at[rows(to * 2 + k)], stage1.at[0, rows(at)], s7.at[d, k], r1.at[0, at], along_x(d))

    def turn_z(p):
        for e in (1, 2, 3, 0):
            x2, y0 = hop2_groups[e]
            group = x2 * 2 + y0
            for k in range(4):
                arrived(stage1.at[p, rows(group * 4 + k)], r1.at[p, group * 4 + k])
            copy = (stage1.at[p, rows(group * 4, 4)], stage2.at[p, rows(slot2 * 4, 4)], s2.at[p, e], r2.at[p, slot2], hop2[e])
            if e:
                start(*copy)
            else:
                start_or_own(turn2, *copy)

    def turn_y(p, to_where, send_sem):
        for slot in range(4):
            arrived(stage2.at[p, rows(slot * 4, 4)], r2.at[p, slot])
        for d in far_first:
            to = (y + d) % 8
            for zl in range(2):
                dst, recv_sem = to_where(zl)
                start_or_copy(d, stage2.at[p, rows((to % 2 * 2 + zl) * 4 + to // 2)], dst, send_sem.at[d, zl], recv_sem, along_y(d))

    def to_far(zl):
        return far.at[rows(y * 2 + zl)], r8.at[y * 2 + zl]

    def to_stage3(zl):
        at = (zl * 4 + y_top) * 2 + y_low
        return stage3.at[rows(at)], r3.at[at]

    def last_x():
        for d in far_first:
            to = (x + d) % 8
            for k in range(2):
                arrived(stage3.at[rows(to * 2 + k)], r3.at[to * 2 + k])
            start_or_copy(d, stage3.at[rows(to * 2, 2)], far.at[rows(PARTS + x * 2, 2)], s6.at[d], r6.at[x], along_x(d))

    def ahead(q):
        return 2 * q * size < next_rows

    spread_x()
    spread_y()
    for n in range(LEFT_FIRST):
        send_left(n)
    turn_z(1)
    cross_x()
    turn_y(1, to_stage3, s3)
    turn_z(0)
    for n in range(LEFT_FIRST, LEFT_PARTS):
        send_left(n)
    last_x()
    turn_y(0, to_far, s8)
    for q in range(PARTS):
        span = rows(2 * q, 2)
        if q < 8:
            for k in range(2):
                arrived(far.at[rows(2 * q + k)], r8.at[2 * q + k])
        else:
            arrived(far.at[span], r6.at[q - 8])
        if ahead(q):
            start(far.at[span], far_next.at[span], s4.at[q], r4.at[q], row_before)
    for n in range(LEFT_PARTS):
        span = pl.ds(n * left_size, left_size)
        arrived(left.at[span], r5.at[n])
    for q in range(PARTS):
        if ahead(q):
            arrived(far_next.at[rows(2 * q, 2)], r4.at[q])
    for made in sends:
        made.wait_send()
    for own, made in turns:
        @pl.when(jnp.logical_not(own))
        def _():
            made.wait_send()


def exchanged(far_src, left_src, far_blocks, left_blocks, next_blocks, collective_id):
    far_rows, left_rows, next_rows = far_blocks * WIDTH, left_blocks * WIDTH, next_blocks * WIDTH
    piece = far_rows // PARTS
    next_rows = -(-next_rows // piece) * piece
    shape = lambda rows: jax.ShapeDtypeStruct((rows, WIDTH), jnp.float32)
    anywhere = pl.BlockSpec(memory_space=pl.ANY)
    dma = pltpu.SemaphoreType.DMA
    return pl.pallas_call(
        functools.partial(exchange, far_rows, left_rows, next_rows),
        out_shape=[shape(far_rows), shape(-(-next_rows // WIDTH) * WIDTH), shape(left_rows)],
        in_specs=[anywhere] * 2,
        out_specs=[anywhere] * 3,
        scratch_shapes=[
            pltpu.VMEM((far_rows // 2, WIDTH), jnp.float32),
            pltpu.VMEM((2, far_rows // 2, WIDTH), jnp.float32),
            pltpu.VMEM((2, far_rows // 2, WIDTH), jnp.float32),
            pltpu.VMEM((far_rows // 2, WIDTH), jnp.float32),
            dma((PARTS,)), dma((PARTS,)),
            dma((PARTS,)), dma((2, PARTS)),
            dma((2, 4)), dma((2, 4)),
            dma((8, 2)), dma((PARTS,)),
            dma((PARTS,)), dma((PARTS,)),
            dma((LEFT_PARTS,)), dma((LEFT_PARTS,)),
            dma((8,)), dma((8,)),
            dma((8, 2)), dma((8, 2)), dma((PARTS,)),
        ],
        name="exchange",
        compiler_params=pltpu.CompilerParams(
            collective_id=collective_id, has_side_effects=True, vmem_limit_bytes=16 * 1024 * 1024
        ),
    )(far_src, left_src)


def bits_of(cols, count):
    bits = small(1 << cols[...])
    group = lax.broadcasted_iota(jnp.int32, (GROUPS, GROUPS * SLOTS), 0)
    slot = lax.broadcasted_iota(jnp.int32, (GROUPS, GROUPS * SLOTS), 1)
    held = jnp.zeros((GROUPS, ROWS * GROUPS), jnp.int32)
    for t in range(SLOTS):
        bit = whole_dot(small((slot == group * SLOTS + t).astype(jnp.int32)), bits, ((1,), (0,)))
        held = held | jnp.where(count[...] > t, bit.astype(jnp.int32), 0)
    return held


def small(a):
    return a.astype(jnp.float32).astype(jnp.bfloat16)


def whole_dot(a, b, dims):
    return lax.dot_general(a, b, (dims, ((), ())), preferred_element_type=jnp.float32)


def ones_in(mask):
    mask = mask - ((mask >> 1) & 0x55)
    mask = (mask & 0x33) + ((mask >> 2) & 0x33)
    return (mask + (mask >> 4)) & 0x0F


def over_rows(join, a):
    lanes = a.shape[1]
    for step in (4, 2, 1):
        a = join(a, pltpu.roll(a, lanes - step, 1))
    return a


def plan(panel_cols, panel_count, product_cols, product_count, own, level, table, left_src, far_src,
         left_need, front_need, rest_need, numbers, sem):
    lanes = ROWS * GROUPS
    held = bits_of(panel_cols, panel_count)
    asked = bits_of(product_cols, product_count)
    held_next = jnp.concatenate([held[1:], held[:1]], axis=0)
    row = lax.broadcasted_iota(jnp.int32, (lanes, lanes), 0)
    col = lax.broadcasted_iota(jnp.int32, (lanes, lanes), 1)
    pick = ((row % GROUPS) * ROWS + row // GROUPS == col).astype(jnp.float32).astype(jnp.bfloat16)
    turned = small(whole_dot(pick, small(held), ((1,), (1,))))
    group = lax.broadcasted_iota(jnp.int32, (GROUPS, lanes), 0)
    lane = lax.broadcasted_iota(jnp.int32, (GROUPS, lanes), 1)
    widen = lambda s: (group == (lane // ROWS + s) % GROUPS).astype(jnp.float32).astype(jnp.bfloat16)
    right = whole_dot(turned, widen(0), ((1,), (0,))).astype(jnp.int32)
    right_next = whole_dot(turned, widen(1), ((1,), (0,))).astype(jnp.int32)
    left = jnp.zeros_like(held)
    fronts = jnp.zeros_like(held)
    unions = jnp.zeros_like(held)
    either = lambda a, b: a | b
    for w in range(ROWS):
        span = slice(w * GROUPS, (w + 1) * GROUPS)
        chosen = ((asked >> w) & 1) == 1
        left = left | jnp.where(chosen, right_next[span], 0)
        front = over_rows(either, jnp.where(chosen, held_next, 0)) & right_next[span]
        rest = over_rows(either, jnp.where(chosen, held, 0)) & right[span]
        front_need[span, :] = front
        rest_need[span, :] = rest
        fronts += ones_in(front)
        unions += ones_in(rest | pltpu.roll(front, ROWS, 1))
    left = left & held_next
    left_need[...] = left
    first = lane % ROWS == 0
    most = lambda a: jnp.max(jnp.where(first, a, 0))
    most_left, most_front, most_union = most(over_rows(jnp.add, ones_in(left))), most(fronts), most(unions)
    reached = 0
    for left_blocks, far_blocks, next_blocks in LEVELS:
        over = (most_left > left_blocks) | (most_union > far_blocks) | (most_front > next_blocks)
        reached += over.astype(jnp.int32)
    level[0] = reached

    i, j = lax.axis_index("row"), lax.axis_index("col")
    after = lambda n: (n + 1) % GROUPS
    before = lambda n: (n + GROUPS - 1) % GROUPS
    for at, source, start, size in (
        (OWN_COLS, panel_cols, j * SLOTS, SLOTS), (LEFT_COLS, panel_cols, after(j) * SLOTS, SLOTS),
        (OWN_COUNT, panel_count, j, 1), (LEFT_COUNT, panel_count, after(j), 1),
        (WANT_COLS, product_cols, j * SLOTS, SLOTS), (WANT_COUNT, product_count, j, 1),
        (FAR_COLS, panel_cols, i * SLOTS, SLOTS), (NEXT_COLS, panel_cols, after(i) * SLOTS, SLOTS),
        (FAR_COUNT, panel_count, i, 1), (NEXT_COUNT, panel_count, after(i), 1),
        (LEFT_OUT, left_need, before(j), 1), (LEFT_IN, left_need, j, 1),
    ):
        for n in range(size):
            table[pl.ds(at + n, 1), :] = source[pl.ds(start + n, 1), :]
    for at, source, start in (
        (FRONT_OUT, front_need, i), (REST_OUT, rest_need, i), (FRONT_IN, front_need, j), (REST_IN, rest_need, j),
    ):
        for w in range(ROWS):
            table[pl.ds(at + w, 1), :] = source[pl.ds(start + w * GROUPS, 1), :]
    copy = pltpu.make_async_copy(table, numbers, sem)
    copy.start()
    copy.wait()

    mine = i * ROWS

    def pack(needed, to, at):
        def one_row(r, at):
            for t in range(SLOTS):
                take = (numbers[OWN_COUNT, mine + r] > t) & (((needed(r) >> numbers[OWN_COLS + t, mine + r]) & 1) == 1)

                @pl.when(take & (at < to.shape[0]))
                def _():
                    to[at] = own[r * SLOTS + t]

                at = at + take.astype(jnp.int32)
            return at

        return lax.fori_loop(0, ROWS, one_row, at)

    front = lambda r: numbers[FRONT_OUT + r, before(j) * ROWS]
    pack(lambda r: numbers[LEFT_OUT, mine + r], left_src, 0)
    pack(lambda r: numbers[REST_OUT + r, j * ROWS] & ~front(r), far_src, pack(front, far_src, 0))


def planned(own, *tables):
    vmem = pl.BlockSpec(memory_space=pltpu.VMEM)
    block = lambda n: jax.ShapeDtypeStruct((n, WIDTH, WIDTH), jnp.float32)
    numbers = (TABLE, ROWS * GROUPS)
    need = pltpu.VMEM((ROWS * GROUPS, ROWS * GROUPS), jnp.int32)
    return pl.pallas_call(
        plan,
        out_shape=[
            jax.ShapeDtypeStruct((1,), jnp.int32), jax.ShapeDtypeStruct(numbers, jnp.int32),
            block(LEVELS[-1][0]), block(LEVELS[-1][1]),
        ],
        in_specs=[vmem] * 5,
        out_specs=[pl.BlockSpec(memory_space=pltpu.SMEM), vmem, vmem, vmem],
        scratch_shapes=[
            pltpu.VMEM((GROUPS, ROWS * GROUPS), jnp.int32), need, need,
            pltpu.SMEM(numbers, jnp.int32), pltpu.SemaphoreType.DMA,
        ],
        name="plan",
        compiler_params=pltpu.CompilerParams(vmem_limit_bytes=32 * 1024 * 1024),
    )(*tables, own)


def multiply(packed, table, own, left, far, far_next, out, places):
    i, j = lax.axis_index("row"), lax.axis_index("col")
    mine, other = i * ROWS, j * ROWS
    out[...] = jnp.zeros_like(out)

    def number(which, count, cols, base, needed, at):
        def one_row(r, at):
            for t in range(SLOTS):
                take = (table[count, base + r] > t) & (((needed(r) >> table[cols + t, base + r]) & 1) == 1)

                @pl.when(take)
                def _():
                    places[which, r * SLOTS + t] = at

                at = at + take.astype(jnp.int32)
            return at

        return lax.fori_loop(0, ROWS, one_row, at)

    if packed:
        front = lambda w: table[FRONT_IN + w, ((i + GROUPS - 1) % GROUPS) * ROWS]
        number(0, LEFT_COUNT, LEFT_COLS, mine, lambda r: table[LEFT_IN, mine + r], 0)
        number(2, NEXT_COUNT, NEXT_COLS, other, lambda w: table[FRONT_IN + w, mine], 0)
        size = number(1, FAR_COUNT, FAR_COLS, other, front, 0)
        number(1, FAR_COUNT, FAR_COLS, other, lambda w: table[REST_IN + w, mine] & ~front(w), size)
    place_of = lambda which, slot: places[which, slot] if packed else slot

    def halves(a):
        high = a.astype(jnp.bfloat16)
        return high, (a - high.astype(jnp.float32)).astype(jnp.bfloat16)

    def term(at, a, b):
        (a_high, a_low), (b_high, b_low) = halves(a), halves(b)
        dot = lambda p, q: whole_dot(p, q, ((1,), (1,)))
        out[at] += dot(a_high, b_high) + (dot(a_high, b_low) + dot(a_low, b_high))

    sides = (
        (OWN_COUNT, OWN_COLS, own, lambda slot: slot, FAR_COUNT, FAR_COLS, far, lambda slot: place_of(1, slot)),
        (LEFT_COUNT, LEFT_COLS, left, lambda slot: place_of(0, slot), NEXT_COUNT, NEXT_COLS, far_next,
         lambda slot: place_of(2, slot)),
    )

    def one_row(r, _):
        def one_slot(q, _):
            c = table[WANT_COLS + q, mine + r]
            for left_count, left_cols, lefts, left_at, right_count, right_cols, rights, right_at in sides:
                def one_left(t, _):
                    m = table[left_cols + t, mine + r]

                    def one_right(k, _):
                        @pl.when(table[right_cols + k, other + c] == m)
                        def _():
                            term(r * SLOTS + q, lefts[left_at(r * SLOTS + t)], rights[right_at(c * SLOTS + k)])
                        return 0

                    return lax.fori_loop(0, table[right_count, other + c], one_right, 0)

                lax.fori_loop(0, table[left_count, mine + r], one_left, 0)
            return 0

        return lax.fori_loop(0, table[WANT_COUNT, mine + r], one_slot, 0)

    lax.fori_loop(0, ROWS, one_row, 0)


def multiplied(packed, table, *arrays):
    vmem = pl.BlockSpec(memory_space=pltpu.VMEM)
    return pl.pallas_call(
        functools.partial(multiply, packed),
        out_shape=jax.ShapeDtypeStruct((BLOCKS, WIDTH, WIDTH), jnp.float32),
        in_specs=[pl.BlockSpec(memory_space=pltpu.SMEM)] + [vmem] * 4,
        out_specs=vmem,
        scratch_shapes=[pltpu.SMEM((3, BLOCKS), jnp.int32)],
        name="multiply",
        compiler_params=pltpu.CompilerParams(vmem_limit_bytes=32 * 1024 * 1024),
    )(table, *(a.reshape(-1, WIDTH, WIDTH) for a in arrays))


def on_device(panel_blocks, panel_cols, panel_count, product_cols, product_count):
    own = panel_blocks.reshape(BLOCKS, WIDTH, WIDTH)
    flat = lambda a: a.reshape(-1, WIDTH)
    level, table, left_src, far_src = planned(own, panel_cols.T, panel_count.T, product_cols.T, product_count.T)

    def at_level(n):
        def run():
            if n < len(LEVELS):
                left_blocks, far_blocks, next_blocks = LEVELS[n]
                sent = exchanged(flat(far_src), flat(left_src), far_blocks, left_blocks, next_blocks, n + 1)
            else:
                sent = exchanged(flat(own), flat(own), BLOCKS, BLOCKS, BLOCKS, n + 1)
            far, far_next, left = sent
            return multiplied(n < len(LEVELS), table, own, left, far, far_next)
        return run

    product = lax.switch(level[0], [at_level(n) for n in range(len(LEVELS) + 1)])
    return product.reshape(ROWS, SLOTS, WIDTH, WIDTH)


def solution(mesh):
    return jax.shard_map(
        on_device,
        mesh=mesh,
        in_specs=(P("row", "col", None, None), P(), P(), P(), P()),
        out_specs=P("row", "col", None, None),
        check_vma=False,
    )
```

```python
import functools

import jax
import jax.numpy as jnp
from jax import lax
from jax.experimental import pallas as pl
from jax.experimental.pallas import tpu as pltpu
from jax.sharding import PartitionSpec as P

WIDTH = 128
ROWS = 8
SLOTS = 3
GROUPS = 32
BLOCKS = ROWS * SLOTS
PARTS = 16
LEFT_PARTS = 4
LEFT_FIRST = 1
LEVELS = ((12, 16, 12), (14, 18, 14))
OWN_COLS, LEFT_COLS, OWN_COUNT, LEFT_COUNT, WANT_COLS, WANT_COUNT = 0, 3, 6, 7, 8, 11
FAR_COLS, NEXT_COLS, FAR_COUNT, NEXT_COUNT, LEFT_OUT, LEFT_IN = 12, 15, 18, 19, 20, 21
FRONT_OUT, REST_OUT, FRONT_IN, REST_IN, TABLE = 24, 32, 40, 48, 56
MESH = pl.DeviceIdType.MESH


def place(x, y, z_hi, z_lo, core):
    return ((z_lo * 8 + y) * 2 + core, x * 4 + z_hi)


def exchange(far_rows, left_rows, next_rows, far_src, left_src, far, far_next, left, stage0, stage1, stage2, stage3,
             s0, r0, s1, r1, s2, r2, s3, r3, s4, r4, s5, r5, s6, r6, s7, s8, r8, held, s9, r9):
    size = far_rows // (2 * PARTS)
    i, j = lax.axis_index("row"), lax.axis_index("col")
    core, y, z_lo = i % 2, (i // 2) % 8, i // 16
    x, z_hi = j // 4, j % 4
    zh1, zh0 = z_hi // 2, z_hi % 2
    x_top, x_low = x // 4, x % 4
    y_top, y_low = y // 2, y % 2
    flip = lambda bit, by: (bit + by) % 2
    turn2 = z_hi % 2 == core

    def hop1(e):
        return place((x + e // 2) % 8, y_top * 2 + flip(y_low, e % 2), z_hi, z_lo, core)

    def hop1_y(e):
        return place(x, (y + e // 2) % 8, z_hi, flip(z_lo, e % 2), core)

    hop2_groups = [(flip(z_lo, e // 2), flip(zh1, e % 2)) for e in range(4)]
    hop2 = [place(x, y, y0 * 2 + core, x2, zh0) for x2, y0 in hop2_groups]
    hop2_from = [place(x, y, flip(zh1, e % 2) * 2 + core, flip(z_lo, e // 2), zh0) for e in range(4)]
    along_y = lambda d: place(x, (y + d) % 8, z_hi, z_lo, core)
    along_x = lambda d: place((x + d) % 8, y, z_hi, z_lo, core)
    row_before = ((i + GROUPS - 1) % GROUPS, j)
    row_after = ((i + 1) % GROUPS, j)
    col_before = (i, (j + GROUPS - 1) % GROUPS)
    col_after = (i, (j + 1) % GROUPS)

    def leg(n, at, to):
        z = (n % 4 * 2 + at + to) % 8
        return place(n // 4, y, z // 2, z % 2, core)

    relay = leg(j, z_lo, 3)
    relayed_by = leg(j, z_lo, 5)
    owner = (z_hi * 2 + z_lo + 5) % 8
    relay_end = (((owner % 2) * 8 + y) * 2 + core, (x * 4 + owner // 2 + GROUPS - 1) % GROUPS)
    relay_mine = leg((j + 1) % GROUPS, z_lo, 3)

    barrier = pltpu.get_barrier_semaphore()

    def greet(to):
        pl.semaphore_signal(barrier, inc=1, device_id=to, device_id_type=MESH)

    for e in range(1, PARTS):
        greet(hop1(e))
        greet(hop1_y(e))
    for sender in hop2_from:
        greet(sender)
    greet(row_after)
    greet(relayed_by)
    greet(relay_mine)
    greet(col_after)
    pl.semaphore_wait(barrier, 2 * (PARTS - 1) + 4 + 4)

    def remote(src, dst, send_sem, recv_sem, to):
        return pltpu.make_async_remote_copy(
            src_ref=src, dst_ref=dst, send_sem=send_sem, recv_sem=recv_sem, device_id=to, device_id_type=MESH
        )

    sends = []
    turns = []

    def start(*copy):
        made = remote(*copy)
        made.start()
        sends.append(made)

    def start_or_own(own, src, dst, send_sem, recv_sem, to):
        made = remote(src, dst, send_sem, recv_sem, to)

        @pl.when(own)
        def _():
            pltpu.make_async_copy(src, dst, recv_sem).start()

        @pl.when(jnp.logical_not(own))
        def _():
            made.start()

        turns.append((own, made))

    def arrived(ref, sem):
        pltpu.make_async_copy(ref, ref, sem).wait()

    left_size = left_rows // LEFT_PARTS

    def send_left(n):
        span = pl.ds(n * left_size, left_size)
        start(left_src.at[span], left.at[span], s5.at[n], r5.at[n], col_before)

    def rows(at, n=1):
        return pl.ds(pl.multiple_of(at * size, 8), n * size)

    slot2 = zh1 * 2 + z_lo
    far_first = (4, 3, 5, 2, 6, 1, 7, 0)

    def start_or_copy(d, src, dst, send_sem, recv_sem, to):
        if d:
            start(src, dst, send_sem, recv_sem, to)
        else:
            pltpu.make_async_copy(src, dst, recv_sem).start()

    def spread_y():
        at = (z_lo * 4 + y_top) * 2 + y_low
        for e in list(range(1, PARTS)) + [0]:
            chunk = ((y + e // 2) % 8) * 2 + flip(z_lo, e % 2)
            start_or_copy(e, far_src.at[rows(chunk)], stage0.at[rows(at)], s0.at[e], r0.at[at], hop1_y(e))

    def spread_x():
        at = (x_top * 2 + y_low) * 4 + x_low
        for e in list(range(1, PARTS)) + [0]:
            chunk = PARTS + ((x + e // 2) % 8) * 2 + flip(y_low, e % 2)
            start_or_copy(e, far_src.at[rows(chunk)], stage1.at[1, rows(at)], s1.at[e], r1.at[1, at], hop1(e))

    def cross_x():
        for d in far_first:
            to = (x + d) % 8
            for k in range(2):
                arrived(stage0.at[rows(to * 2 + k)], r0.at[to * 2 + k])
                at = (x_top * 2 + k) * 4 + x_low
                start_or_copy(d, stage0.at[rows(to * 2 + k)], stage1.at[0, rows(at)], s7.at[d, k], r1.at[0, at], along_x(d))

    def turn_z(p):
        for e in (1, 2, 3, 0):
            x2, y0 = hop2_groups[e]
            group = x2 * 2 + y0
            for k in range(4):
                arrived(stage1.at[p, rows(group * 4 + k)], r1.at[p, group * 4 + k])
            copy = (stage1.at[p, rows(group * 4, 4)], stage2.at[p, rows(slot2 * 4, 4)], s2.at[p, e], r2.at[p, slot2], hop2[e])
            if e:
                start(*copy)
            else:
                start_or_own(turn2, *copy)

    def turn_y(p, to_where, send_sem):
        for slot in range(4):
            arrived(stage2.at[p, rows(slot * 4, 4)], r2.at[p, slot])
        for d in far_first:
            to = (y + d) % 8
            for zl in range(2):
                dst, recv_sem = to_where(zl)
                start_or_copy(d, stage2.at[p, rows((to % 2 * 2 + zl) * 4 + to // 2)], dst, send_sem.at[d, zl], recv_sem, along_y(d))

    def to_far(zl):
        return far.at[rows(y * 2 + zl)], r8.at[y * 2 + zl]

    def to_stage3(zl):
        at = (zl * 4 + y_top) * 2 + y_low
        return stage3.at[rows(at)], r3.at[at]

    def last_x():
        for d in far_first:
            to = (x + d) % 8
            for k in range(2):
                arrived(stage3.at[rows(to * 2 + k)], r3.at[to * 2 + k])
            start_or_copy(d, stage3.at[rows(to * 2, 2)], far.at[rows(PARTS + x * 2, 2)], s6.at[d], r6.at[x], along_x(d))

    def ahead(q):
        return 2 * q * size < next_rows

    last = LEFT_PARTS - 1
    tail = pl.ds(last * left_size, left_size)
    start(left_src.at[tail], held, s9, r9, relay)
    spread_x()
    spread_y()
    for n in range(LEFT_FIRST):
        send_left(n)
    turn_z(1)
    cross_x()
    turn_y(1, to_stage3, s3)
    turn_z(0)
    arrived(held, r9)
    start(held, left.at[tail], s5.at[last], r5.at[last], relay_end)
    for n in range(LEFT_FIRST, last):
        send_left(n)
    last_x()
    turn_y(0, to_far, s8)
    for q in range(PARTS):
        span = rows(2 * q, 2)
        if q < 8:
            for k in range(2):
                arrived(far.at[rows(2 * q + k)], r8.at[2 * q + k])
        else:
            arrived(far.at[span], r6.at[q - 8])
        if ahead(q):
            start(far.at[span], far_next.at[span], s4.at[q], r4.at[q], row_before)
    for n in range(LEFT_PARTS):
        span = pl.ds(n * left_size, left_size)
        arrived(left.at[span], r5.at[n])
    for q in range(PARTS):
        if ahead(q):
            arrived(far_next.at[rows(2 * q, 2)], r4.at[q])
    for made in sends:
        made.wait_send()
    for own, made in turns:
        @pl.when(jnp.logical_not(own))
        def _():
            made.wait_send()


def exchanged(far_src, left_src, far_blocks, left_blocks, next_blocks, collective_id):
    far_rows, left_rows, next_rows = far_blocks * WIDTH, left_blocks * WIDTH, next_blocks * WIDTH
    piece = far_rows // PARTS
    next_rows = -(-next_rows // piece) * piece
    shape = lambda rows: jax.ShapeDtypeStruct((rows, WIDTH), jnp.float32)
    anywhere = pl.BlockSpec(memory_space=pl.ANY)
    dma = pltpu.SemaphoreType.DMA
    return pl.pallas_call(
        functools.partial(exchange, far_rows, left_rows, next_rows),
        out_shape=[shape(far_rows), shape(-(-next_rows // WIDTH) * WIDTH), shape(left_rows)],
        in_specs=[anywhere] * 2,
        out_specs=[anywhere] * 3,
        scratch_shapes=[
            pltpu.VMEM((far_rows // 2, WIDTH), jnp.float32),
            pltpu.VMEM((2, far_rows // 2, WIDTH), jnp.float32),
            pltpu.VMEM((2, far_rows // 2, WIDTH), jnp.float32),
            pltpu.VMEM((far_rows // 2, WIDTH), jnp.float32),
            dma((PARTS,)), dma((PARTS,)),
            dma((PARTS,)), dma((2, PARTS)),
            dma((2, 4)), dma((2, 4)),
            dma((8, 2)), dma((PARTS,)),
            dma((PARTS,)), dma((PARTS,)),
            dma((LEFT_PARTS,)), dma((LEFT_PARTS,)),
            dma((8,)), dma((8,)),
            dma((8, 2)), dma((8, 2)), dma((PARTS,)),
            pltpu.VMEM((left_rows // LEFT_PARTS, WIDTH), jnp.float32), dma, dma,
        ],
        name="exchange",
        compiler_params=pltpu.CompilerParams(
            collective_id=collective_id, has_side_effects=True, vmem_limit_bytes=16 * 1024 * 1024
        ),
    )(far_src, left_src)


def bits_of(cols, count):
    bits = small(1 << cols[...])
    group = lax.broadcasted_iota(jnp.int32, (GROUPS, GROUPS * SLOTS), 0)
    slot = lax.broadcasted_iota(jnp.int32, (GROUPS, GROUPS * SLOTS), 1)
    held = jnp.zeros((GROUPS, ROWS * GROUPS), jnp.int32)
    for t in range(SLOTS):
        bit = whole_dot(small((slot == group * SLOTS + t).astype(jnp.int32)), bits, ((1,), (0,)))
        held = held | jnp.where(count[...] > t, bit.astype(jnp.int32), 0)
    return held


def small(a):
    return a.astype(jnp.float32).astype(jnp.bfloat16)


def whole_dot(a, b, dims):
    return lax.dot_general(a, b, (dims, ((), ())), preferred_element_type=jnp.float32)


def ones_in(mask):
    mask = mask - ((mask >> 1) & 0x55)
    mask = (mask & 0x33) + ((mask >> 2) & 0x33)
    return (mask + (mask >> 4)) & 0x0F


def over_rows(join, a):
    lanes = a.shape[1]
    for step in (4, 2, 1):
        a = join(a, pltpu.roll(a, lanes - step, 1))
    return a


def plan(panel_cols, panel_count, product_cols, product_count, own, level, table, left_src, far_src,
         left_need, front_need, rest_need, numbers, sem):
    lanes = ROWS * GROUPS
    held = bits_of(panel_cols, panel_count)
    asked = bits_of(product_cols, product_count)
    held_next = jnp.concatenate([held[1:], held[:1]], axis=0)
    row = lax.broadcasted_iota(jnp.int32, (lanes, lanes), 0)
    col = lax.broadcasted_iota(jnp.int32, (lanes, lanes), 1)
    pick = ((row % GROUPS) * ROWS + row // GROUPS == col).astype(jnp.float32).astype(jnp.bfloat16)
    turned = small(whole_dot(pick, small(held), ((1,), (1,))))
    group = lax.broadcasted_iota(jnp.int32, (GROUPS, lanes), 0)
    lane = lax.broadcasted_iota(jnp.int32, (GROUPS, lanes), 1)
    widen = lambda s: (group == (lane // ROWS + s) % GROUPS).astype(jnp.float32).astype(jnp.bfloat16)
    right = whole_dot(turned, widen(0), ((1,), (0,))).astype(jnp.int32)
    right_next = whole_dot(turned, widen(1), ((1,), (0,))).astype(jnp.int32)
    left = jnp.zeros_like(held)
    fronts = jnp.zeros_like(held)
    unions = jnp.zeros_like(held)
    either = lambda a, b: a | b
    for w in range(ROWS):
        span = slice(w * GROUPS, (w + 1) * GROUPS)
        chosen = ((asked >> w) & 1) == 1
        left = left | jnp.where(chosen, right_next[span], 0)
        front = over_rows(either, jnp.where(chosen, held_next, 0)) & right_next[span]
        rest = over_rows(either, jnp.where(chosen, held, 0)) & right[span]
        front_need[span, :] = front
        rest_need[span, :] = rest
        fronts += ones_in(front)
        unions += ones_in(rest | pltpu.roll(front, ROWS, 1))
    left = left & held_next
    left_need[...] = left
    first = lane % ROWS == 0
    most = lambda a: jnp.max(jnp.where(first, a, 0))
    most_left, most_front, most_union = most(over_rows(jnp.add, ones_in(left))), most(fronts), most(unions)
    reached = 0
    for left_blocks, far_blocks, next_blocks in LEVELS:
        over = (most_left > left_blocks) | (most_union > far_blocks) | (most_front > next_blocks)
        reached += over.astype(jnp.int32)
    level[0] = reached

    i, j = lax.axis_index("row"), lax.axis_index("col")
    after = lambda n: (n + 1) % GROUPS
    before = lambda n: (n + GROUPS - 1) % GROUPS
    for at, source, start, size in (
        (OWN_COLS, panel_cols, j * SLOTS, SLOTS), (LEFT_COLS, panel_cols, after(j) * SLOTS, SLOTS),
        (OWN_COUNT, panel_count, j, 1), (LEFT_COUNT, panel_count, after(j), 1),
        (WANT_COLS, product_cols, j * SLOTS, SLOTS), (WANT_COUNT, product_count, j, 1),
        (FAR_COLS, panel_cols, i * SLOTS, SLOTS), (NEXT_COLS, panel_cols, after(i) * SLOTS, SLOTS),
        (FAR_COUNT, panel_count, i, 1), (NEXT_COUNT, panel_count, after(i), 1),
        (LEFT_OUT, left_need, before(j), 1), (LEFT_IN, left_need, j, 1),
    ):
        for n in range(size):
            table[pl.ds(at + n, 1), :] = source[pl.ds(start + n, 1), :]
    for at, source, start in (
        (FRONT_OUT, front_need, i), (REST_OUT, rest_need, i), (FRONT_IN, front_need, j), (REST_IN, rest_need, j),
    ):
        for w in range(ROWS):
            table[pl.ds(at + w, 1), :] = source[pl.ds(start + w * GROUPS, 1), :]
    copy = pltpu.make_async_copy(table, numbers, sem)
    copy.start()
    copy.wait()

    mine = i * ROWS

    def pack(needed, to, at):
        def one_row(r, at):
            for t in range(SLOTS):
                take = (numbers[OWN_COUNT, mine + r] > t) & (((needed(r) >> numbers[OWN_COLS + t, mine + r]) & 1) == 1)

                @pl.when(take & (at < to.shape[0]))
                def _():
                    to[at] = own[r * SLOTS + t]

                at = at + take.astype(jnp.int32)
            return at

        return lax.fori_loop(0, ROWS, one_row, at)

    front = lambda r: numbers[FRONT_OUT + r, before(j) * ROWS]
    pack(lambda r: numbers[LEFT_OUT, mine + r], left_src, 0)
    pack(lambda r: numbers[REST_OUT + r, j * ROWS] & ~front(r), far_src, pack(front, far_src, 0))


def planned(own, *tables):
    vmem = pl.BlockSpec(memory_space=pltpu.VMEM)
    block = lambda n: jax.ShapeDtypeStruct((n, WIDTH, WIDTH), jnp.float32)
    numbers = (TABLE, ROWS * GROUPS)
    need = pltpu.VMEM((ROWS * GROUPS, ROWS * GROUPS), jnp.int32)
    return pl.pallas_call(
        plan,
        out_shape=[
            jax.ShapeDtypeStruct((1,), jnp.int32), jax.ShapeDtypeStruct(numbers, jnp.int32),
            block(LEVELS[-1][0]), block(LEVELS[-1][1]),
        ],
        in_specs=[vmem] * 5,
        out_specs=[pl.BlockSpec(memory_space=pltpu.SMEM), vmem, vmem, vmem],
        scratch_shapes=[
            pltpu.VMEM((GROUPS, ROWS * GROUPS), jnp.int32), need, need,
            pltpu.SMEM(numbers, jnp.int32), pltpu.SemaphoreType.DMA,
        ],
        name="plan",
        compiler_params=pltpu.CompilerParams(vmem_limit_bytes=32 * 1024 * 1024),
    )(*tables, own)


def multiply(packed, table, own, left, far, far_next, out, places):
    i, j = lax.axis_index("row"), lax.axis_index("col")
    mine, other = i * ROWS, j * ROWS
    out[...] = jnp.zeros_like(out)

    def number(which, count, cols, base, needed, at):
        def one_row(r, at):
            for t in range(SLOTS):
                take = (table[count, base + r] > t) & (((needed(r) >> table[cols + t, base + r]) & 1) == 1)

                @pl.when(take)
                def _():
                    places[which, r * SLOTS + t] = at

                at = at + take.astype(jnp.int32)
            return at

        return lax.fori_loop(0, ROWS, one_row, at)

    if packed:
        front = lambda w: table[FRONT_IN + w, ((i + GROUPS - 1) % GROUPS) * ROWS]
        number(0, LEFT_COUNT, LEFT_COLS, mine, lambda r: table[LEFT_IN, mine + r], 0)
        number(2, NEXT_COUNT, NEXT_COLS, other, lambda w: table[FRONT_IN + w, mine], 0)
        size = number(1, FAR_COUNT, FAR_COLS, other, front, 0)
        number(1, FAR_COUNT, FAR_COLS, other, lambda w: table[REST_IN + w, mine] & ~front(w), size)
    place_of = lambda which, slot: places[which, slot] if packed else slot

    def halves(a):
        high = a.astype(jnp.bfloat16)
        return high, (a - high.astype(jnp.float32)).astype(jnp.bfloat16)

    def term(at, a, b):
        (a_high, a_low), (b_high, b_low) = halves(a), halves(b)
        dot = lambda p, q: whole_dot(p, q, ((1,), (1,)))
        out[at] += dot(a_high, b_high) + (dot(a_high, b_low) + dot(a_low, b_high))

    sides = (
        (OWN_COUNT, OWN_COLS, own, lambda slot: slot, FAR_COUNT, FAR_COLS, far, lambda slot: place_of(1, slot)),
        (LEFT_COUNT, LEFT_COLS, left, lambda slot: place_of(0, slot), NEXT_COUNT, NEXT_COLS, far_next,
         lambda slot: place_of(2, slot)),
    )

    def one_row(r, _):
        def one_slot(q, _):
            c = table[WANT_COLS + q, mine + r]
            for left_count, left_cols, lefts, left_at, right_count, right_cols, rights, right_at in sides:
                def one_left(t, _):
                    m = table[left_cols + t, mine + r]

                    def one_right(k, _):
                        @pl.when(table[right_cols + k, other + c] == m)
                        def _():
                            term(r * SLOTS + q, lefts[left_at(r * SLOTS + t)], rights[right_at(c * SLOTS + k)])
                        return 0

                    return lax.fori_loop(0, table[right_count, other + c], one_right, 0)

                lax.fori_loop(0, table[left_count, mine + r], one_left, 0)
            return 0

        return lax.fori_loop(0, table[WANT_COUNT, mine + r], one_slot, 0)

    lax.fori_loop(0, ROWS, one_row, 0)


def multiplied(packed, table, *arrays):
    vmem = pl.BlockSpec(memory_space=pltpu.VMEM)
    return pl.pallas_call(
        functools.partial(multiply, packed),
        out_shape=jax.ShapeDtypeStruct((BLOCKS, WIDTH, WIDTH), jnp.float32),
        in_specs=[pl.BlockSpec(memory_space=pltpu.SMEM)] + [vmem] * 4,
        out_specs=vmem,
        scratch_shapes=[pltpu.SMEM((3, BLOCKS), jnp.int32)],
        name="multiply",
        compiler_params=pltpu.CompilerParams(vmem_limit_bytes=32 * 1024 * 1024),
    )(table, *(a.reshape(-1, WIDTH, WIDTH) for a in arrays))


def on_device(panel_blocks, panel_cols, panel_count, product_cols, product_count):
    own = panel_blocks.reshape(BLOCKS, WIDTH, WIDTH)
    flat = lambda a: a.reshape(-1, WIDTH)
    level, table, left_src, far_src = planned(own, panel_cols.T, panel_count.T, product_cols.T, product_count.T)

    def at_level(n):
        def run():
            if n < len(LEVELS):
                left_blocks, far_blocks, next_blocks = LEVELS[n]
                sent = exchanged(flat(far_src), flat(left_src), far_blocks, left_blocks, next_blocks, n + 1)
            else:
                sent = exchanged(flat(own), flat(own), BLOCKS, BLOCKS, BLOCKS, n + 1)
            far, far_next, left = sent
            return multiplied(n < len(LEVELS), table, own, left, far, far_next)
        return run

    product = lax.switch(level[0], [at_level(n) for n in range(len(LEVELS) + 1)])
    return product.reshape(ROWS, SLOTS, WIDTH, WIDTH)


def solution(mesh):
    return jax.shard_map(
        on_device,
        mesh=mesh,
        in_specs=(P("row", "col", None, None), P(), P(), P(), P()),
        out_specs=P("row", "col", None, None),
        check_vma=False,
    )
```
